256 devices in a mesh: expert: 8 (over z), context: 32 (over y, x, core).
Axes of the slice: x: 4, y: 4, z: 8, core: 2. Of those that a mesh axis runs over, the one named last changes fastest.
Arguments:
- hidden: bfloat16 [4096, 2048], P('context'), may hold values from -6 to 6
- upstream: bfloat16 [4096, 2048], P('context'), may hold values from -6 to 6
- norm_gain: float32 [2048], replicated, may hold values from 0.5 to 1.5
- route_ids: int32 [4096, 8], P('context'), may hold values from 0 to 127, all different within a row; in each aligned block of 128 rows (0 to 127, 128 to 255, ...) at most 12 rows name the same one
- route_weights: bfloat16 [4096, 8], P('context'), may hold values from 0.049804688 to 0.29882812
- w_gate: bfloat16 [128, 2048, 1024], P('context', None, 'expert'), may hold values from -0.125 to 0.125
- w_up: bfloat16 [128, 2048, 1024], P('context', None, 'expert'), may hold values from -0.125 to 0.125
- w_down: bfloat16 [128, 1024, 2048], P('context', 'expert'), may hold values from -0.1875 to 0.1875
- w_out: bfloat16 [2048, 2048], P('expert'), may hold values from -0.125 to 0.125
- queries: bfloat16 [4096, 2048], P('context', 'expert'), may hold values from -48 to 48
- keys: bfloat16 [4096, 256], P('context'), may hold values from -4 to 4
- values: bfloat16 [4096, 256], P('context'), may hold values from -6 to 6
Outputs:
- d_hidden: bfloat16 [4096, 2048], P('context')
- d_route: float32 [4096, 8], P('context')
- d_queries: float32 [4096, 2048], P('context', 'expert')
- d_keys: float32 [4096, 256], P('context')
- d_values: float32 [4096, 256], P('context')
The draws below stay inside these ranges and needn't reach their ends.
Inputs may be any that keep to these rules, and one draw needn't show every extreme that they name: `route_ids`: in each aligned block of 128 rows, no expert is named by more than 12 rows, a bound that some block reaches.
All inputs are finite; a program needn't handle non-finite values.
Results may differ from the reference program's by a relative error of at most 0.015.
Values may be sent and summed in bfloat16 or wider, within the bound.
No kernel may reach another device: no remote copies, remote signals or barrier semaphores. Data moves between devices by JAX's collectives and lax.ppermute only.
A program may use at most 128 MiB of HBM per device.

```python
import math
import jax
import jax.numpy as jnp
import numpy as np
from jax import lax

SEQ_DEV = 128
SEQ = 4096
D = 2048
HEADS = 16
KV_HEADS = 2
HEAD_DIM = 128
EXPERTS = 128
TOPK = 8
FF = 1024
CAP = 12
N_EXPERT = 8
N_CONTEXT = 32


def shared_keys(key):
    return jnp.clip(jax.random.normal(key, (SEQ, KV_HEADS * HEAD_DIM), jnp.float32), -4.0, 4.0)


def draw_keys(key, part):
    shared = shared_keys(key)
    return shared.astype(jnp.bfloat16)


def draw_queries(key, part):
    key = jax.random.fold_in(key, 12)
    drawn = jnp.clip(jax.random.normal(key, (SEQ, HEADS, HEAD_DIM), jnp.float32), -4.0, 4.0)
    return drawn.reshape(SEQ, HEADS * HEAD_DIM).astype(jnp.bfloat16)


def levels(key, dims, shards, low, top_value):
    def one(axis_at, parts):
        draws = jax.random.uniform(jax.random.fold_in(jax.random.fold_in(key, 6), axis_at), (parts,), jnp.float32, low / len(shards), top_value / len(shards))
        return jnp.repeat(jnp.exp(draws), dims[axis_at] // parts).reshape((-1,) + (1,) * (len(dims) - axis_at - 1))

    level = one(*shards[0])
    for cut in shards[1:]:
        level = level * one(*cut)
    return level


def routed_block(stream_key, own, number, rows, number_of, top, bound, skew):
    order = jax.random.permutation(stream_key, number_of)
    crowded, ordinary = shares(number_of, rows * top, bound, skew, True), shares(number_of, rows * top, bound, skew, False)
    places = jnp.arange(number_of)

    def named(tallies, offset_by):
        used = int((tallies > 0).sum())
        fixed = max(1, used // 4)
        moved = fixed + (places - fixed + offset_by * (used - fixed)) % max(1, number_of - fixed)
        return jnp.zeros((number_of,), jnp.int32).at[order[jnp.where(places < fixed, places, moved)]].set(jnp.asarray(tallies, jnp.int32))

    tallies = jnp.where(number % 4 == 0, named(crowded, number // 4), named(ordinary, number - number // 4 - 1))
    mixed = jax.random.permutation(jax.random.fold_in(own, 3), number_of)
    giver, taker = mixed[0:number_of // 2 * 2:2], mixed[1:number_of // 2 * 2:2]
    margin = jnp.minimum(tallies[giver] - 1, bound - tallies[taker]) // 2
    margin = jnp.where((giver == order[0]) | (taker == order[0]) | (tallies[taker] == 0), 0, jnp.maximum(margin, 0))
    moved = jax.random.randint(jax.random.fold_in(own, 4), (number_of // 2,), 0, 1 << 20) % (margin + 1)
    tallies = tallies.at[giver].add(-moved).at[taker].add(moved)
    items = jnp.searchsorted(jnp.cumsum(tallies), jnp.arange(rows * top), side="right").astype(jnp.int32)
    table = items.reshape(top, rows).T
    table = table[jax.random.permutation(jax.random.fold_in(own, 1), rows)]
    offset_by = jax.random.randint(jax.random.fold_in(own, 2), (rows, 1), 0, top)
    return jnp.take_along_axis(table, (jnp.arange(top)[None, :] + offset_by) % top, axis=1)


def shares(number_of, total, bound, lean, full):
    weights = [(1 << 20) // math.isqrt(rank ** lean) + 1 for rank in range(1, number_of + 1)]
    largest = bound if full else min(bound, max(-(-total // number_of), total * weights[0] // sum(weights)))
    least = 1 if total - largest >= number_of - 1 else 0
    counts, surplus = [largest] + [least] * (number_of - 1), total - largest - least * (number_of - 1)
    while surplus > 0:
        movable = [i for i in range(1, number_of) if counts[i] < largest] or [i for i in range(1, number_of) if counts[i] < bound]
        mass, budget = sum([weights[i] for i in movable]), surplus
        for i in movable:
            extra = min(bound - counts[i], max(1, budget * weights[i] // mass), surplus)
            counts[i] = counts[i] + extra
            surplus = surplus - extra
    return np.array(counts)


def normal_values(own_key, dims, scale, most, split=(), kind=jnp.bfloat16):
    values = jax.random.normal(own_key, dims, jnp.float32) * scale
    if len(split) > 0:
        values = levels(own_key, dims, split, -0.22, 0.18) * values
    return jnp.clip(values, min=-most, max=most).astype(kind)


def setup_inputs(seed: int = 0) -> dict:
    arg_keys = jax.random.split(jax.random.key(seed), 13)
    hidden = normal_values(arg_keys[0], (SEQ, D), 1.0, 6.0, ((0, 32),))
    upstream = normal_values(arg_keys[1], (SEQ, D), 1.0, 6.0, ((0, 32),))
    norm_gain = jnp.clip(1.0 + 0.1 * jax.random.normal(arg_keys[2], (D,), jnp.float32), 0.5, 1.5)
    route_ids_keys = jax.random.split(jax.random.fold_in(arg_keys[3], 1), SEQ // SEQ_DEV)
    route_ids_turns = jax.random.permutation(jax.random.fold_in(arg_keys[3], 3), SEQ // SEQ_DEV)
    route_ids = jax.vmap(lambda own, number: routed_block(jax.random.fold_in(arg_keys[3], 2), own, number, SEQ_DEV, EXPERTS, TOPK, CAP, 1))(route_ids_keys, route_ids_turns).reshape((SEQ, TOPK))
    route_weights = jnp.clip(0.049804688 + 0.24902344 * jax.random.uniform(arg_keys[4], (SEQ, TOPK), jnp.float32) ** levels(arg_keys[4], (SEQ, TOPK), ((0, 32),), -0.2, 0.2), 0.049804688, 0.29882812).astype(jnp.bfloat16)
    w_gate = normal_values(arg_keys[5], (EXPERTS, D, FF), D ** -0.5, 0.125, ((0, 32), (2, 8)))
    w_up = normal_values(arg_keys[6], (EXPERTS, D, FF), D ** -0.5, 0.125, ((0, 32), (2, 8)))
    w_down = normal_values(arg_keys[7], (EXPERTS, FF, D), FF ** -0.5, 0.1875, ((0, 32), (1, 8)))
    w_out = normal_values(arg_keys[8], (HEADS * HEAD_DIM, D), (HEADS * HEAD_DIM) ** -0.5, 0.125, ((0, 8),))
    queries = draw_queries(jax.random.fold_in(arg_keys[12], 71), 0)
    keys = draw_keys(jax.random.fold_in(arg_keys[12], 71), 0)
    values = normal_values(arg_keys[11], (SEQ, KV_HEADS * HEAD_DIM), 1.0, 6.0, ((0, 32),))
    return dict(hidden=hidden, upstream=upstream, norm_gain=norm_gain, route_ids=route_ids, route_weights=route_weights, w_gate=w_gate, w_up=w_up, w_down=w_down, w_out=w_out, queries=queries, keys=keys, values=values)


def silu_slope(pre_act):
    sigmoid = jax.nn.sigmoid(pre_act)
    return sigmoid * (1.0 + pre_act * (1.0 - sigmoid))

def moe_grads(normed, upstream, route_ids, route_weights, w_gate, w_up, w_down):
    route_total = SEQ * TOPK
    slice_width = FF // N_EXPERT
    shard_ids = route_ids.reshape(N_CONTEXT, SEQ_DEV * TOPK).astype(jnp.int32)
    one_hot = (shard_ids[:, :, None] == jnp.arange(EXPERTS, dtype=jnp.int32)[None, None, :]).astype(jnp.int32)
    slot_rank = lax.optimization_barrier(jnp.sum(jnp.cumsum(one_hot, axis=1) * one_hot, axis=2)) - 1
    column = (jnp.arange(N_CONTEXT, dtype=jnp.int32)[:, None] * CAP + slot_rank).astype(jnp.int32)
    route_index = jnp.arange(route_total, dtype=jnp.int32).reshape(N_CONTEXT, SEQ_DEV * TOPK)
    table = jnp.full((EXPERTS, N_CONTEXT * CAP), route_total, jnp.int32).at[shard_ids, column].set(route_index)
    weights_flat = route_weights.reshape(-1).astype(jnp.float32)

    def step(carry_sums, expert_index):
        rows_sum, weight_sum = carry_sums
        route = table[expert_index]
        valid_slot = route < route_total
        safe_route = jnp.where(valid_slot, route, 0).astype(jnp.int32)
        token = (safe_route // TOPK).astype(jnp.int32)
        weight = jnp.where(valid_slot, weights_flat[safe_route], 0.0)
        rows_in = jnp.where(valid_slot[:, None], normed[token], jnp.zeros_like(normed[token]))
        grad_in = jnp.where(valid_slot[:, None], upstream[token], jnp.zeros_like(upstream[token]))
        gate_w = w_gate[expert_index]
        up_w = w_up[expert_index]
        down_w = w_down[expert_index]
        gate_pre = jnp.dot(rows_in, gate_w, preferred_element_type=jnp.float32)
        up_proj = jnp.dot(rows_in, up_w, preferred_element_type=jnp.float32)
        active = jax.nn.silu(gate_pre)
        product = (active * up_proj).astype(jnp.bfloat16)
        scaled = (weight[:, None] * grad_in.astype(jnp.float32)).astype(jnp.bfloat16)
        d_product = jnp.dot(scaled, down_w.T, preferred_element_type=jnp.float32)
        d_gate = (d_product * up_proj * silu_slope(gate_pre)).astype(jnp.bfloat16)
        d_up = (d_product * active).astype(jnp.bfloat16)
        row_count = rows_in.shape[0]
        gate_sl = d_gate.astype(jnp.float32).reshape(row_count, N_EXPERT, slice_width)
        up_sl = d_up.astype(jnp.float32).reshape(row_count, N_EXPERT, slice_width)
        gate_ws = gate_w.astype(jnp.float32).reshape(D, N_EXPERT, slice_width)
        up_ws = up_w.astype(jnp.float32).reshape(D, N_EXPERT, slice_width)
        pieces = jnp.einsum('rnf,dnf->nrd', gate_sl, gate_ws) + jnp.einsum('rnf,dnf->nrd', up_sl, up_ws)
        pieces_low = lax.optimization_barrier(pieces.astype(jnp.bfloat16))
        d_rows = lax.optimization_barrier(jnp.sum(pieces_low.astype(jnp.float32), axis=0))
        projected = jnp.dot(grad_in, down_w.T, preferred_element_type=jnp.float32)
        route_terms = (product.astype(jnp.float32) * projected).reshape(row_count, N_EXPERT, slice_width)
        route_low = lax.optimization_barrier(lax.optimization_barrier(jnp.sum(route_terms, axis=2)).astype(jnp.bfloat16))
        d_weight = lax.optimization_barrier(jnp.sum(route_low.astype(jnp.float32), axis=1))
        rows_sum = rows_sum.at[token].add(jnp.where(valid_slot[:, None], d_rows, 0.0))
        weight_sum = weight_sum.at[safe_route].add(jnp.where(valid_slot, d_weight, 0.0))
        return ((rows_sum, weight_sum), None)
    start = (jnp.zeros((SEQ, D), jnp.float32), jnp.zeros((route_total,), jnp.float32))
    (rows_sum, weight_sum), unused = lax.scan(step, start, jnp.arange(EXPERTS, dtype=jnp.int32))
    return (rows_sum, weight_sum.reshape(SEQ, TOPK))

def attention_grads(queries, keys, values, d_out):
    group_size = HEADS // KV_HEADS
    score_scale = 1.0 / math.sqrt(HEAD_DIM)
    query_heads = queries.reshape(SEQ, HEADS, HEAD_DIM).transpose(1, 0, 2)
    grad_heads = d_out.reshape(SEQ, HEADS, HEAD_DIM).transpose(1, 0, 2)
    key_heads = keys.reshape(SEQ, KV_HEADS, HEAD_DIM).transpose(1, 0, 2)
    value_heads = values.reshape(SEQ, KV_HEADS, HEAD_DIM).transpose(1, 0, 2)

    def one_head(head):
        query = query_heads[head]
        grad_out = grad_heads[head]
        key_rows = key_heads[head // group_size]
        value_rows = value_heads[head // group_size]
        scores = score_scale * jnp.dot(query, key_rows.T, preferred_element_type=jnp.float32)
        row_max = lax.optimization_barrier(jnp.max(scores, axis=1, keepdims=True))
        shifted = jnp.exp(scores - row_max)
        softmax = shifted / lax.optimization_barrier(jnp.sum(shifted, axis=1, keepdims=True))
        softmax_low = softmax.astype(jnp.bfloat16)
        d_soft = jnp.dot(grad_out, value_rows.T, preferred_element_type=jnp.float32)
        delta = lax.optimization_barrier(jnp.sum(softmax * d_soft, axis=1, keepdims=True))
        d_scores = (softmax * (d_soft - delta)).astype(jnp.bfloat16)
        d_query = score_scale * jnp.dot(d_scores, key_rows, preferred_element_type=jnp.float32)
        d_key = score_scale * jnp.dot(d_scores.T, query, preferred_element_type=jnp.float32)
        d_value = jnp.dot(softmax_low.T, grad_out, preferred_element_type=jnp.float32)
        return (d_query, d_key, d_value)
    d_query, d_key, d_value = lax.map(one_head, jnp.arange(HEADS, dtype=jnp.int32))
    d_queries = d_query.transpose(1, 0, 2).reshape(SEQ, HEADS * HEAD_DIM)
    d_keys = lax.optimization_barrier(jnp.sum(d_key.reshape(KV_HEADS, group_size, SEQ, HEAD_DIM), axis=1))
    d_values = lax.optimization_barrier(jnp.sum(d_value.reshape(KV_HEADS, group_size, SEQ, HEAD_DIM), axis=1))
    d_keys = d_keys.transpose(1, 0, 2).reshape(SEQ, KV_HEADS * HEAD_DIM)
    d_values = d_values.transpose(1, 0, 2).reshape(SEQ, KV_HEADS * HEAD_DIM)
    return (d_queries, d_keys, d_values)

def reference(hidden, upstream, norm_gain, route_ids, route_weights, w_gate, w_up, w_down, w_out, queries, keys, values):
    hidden_wide = hidden.astype(jnp.float32)
    inv_rms = lax.rsqrt(lax.optimization_barrier(jnp.mean(hidden_wide * hidden_wide, axis=1, keepdims=True)) + 1e-06)
    normed = (hidden_wide * inv_rms * norm_gain).astype(jnp.bfloat16)
    d_normed, d_route = moe_grads(normed, upstream, route_ids, route_weights, w_gate, w_up, w_down)
    gained = d_normed * norm_gain
    inner = lax.optimization_barrier(jnp.mean(gained * hidden_wide, axis=1, keepdims=True))
    d_hidden = (upstream.astype(jnp.float32) + inv_rms * gained - hidden_wide * inv_rms * inv_rms * inv_rms * inner).astype(jnp.bfloat16)
    d_out = jnp.dot(d_hidden, w_out.T, preferred_element_type=jnp.float32).astype(jnp.bfloat16)
    d_queries, d_keys, d_values = attention_grads(queries, keys, values, d_out)
    return (d_hidden, d_route, d_queries, d_keys, d_values)
```

```python
import math

import jax
import jax.numpy as jnp
from jax import lax
from jax.experimental import pallas as pl
from jax.experimental.pallas import tpu as pltpu
from jax.sharding import PartitionSpec as P

HEAD_DIM = 128
CAP = 12
PAIR = 2 * CAP
EPS = 1e-06
BF = jnp.bfloat16
F32 = jnp.float32
SCALE = 1.0 / math.sqrt(HEAD_DIM)
NT = (((1,), (1,)), ((), ()))
TN = (((0,), (0,)), ((), ()))
MB = 1 << 20


def nt(a, b):
    return lax.dot_general(a, b, NT, preferred_element_type=F32)


def tn(a, b):
    return lax.dot_general(a, b, TN, preferred_element_type=F32)


def nn(a, b):
    return jnp.dot(a, b, preferred_element_type=F32)


def params(mib=60):
    return pltpu.CompilerParams(vmem_limit_bytes=mib * MB)


def whole(shape):
    return pl.BlockSpec(shape, lambda *_: (0,) * len(shape))


def lane_expert(quarter, per, count, shape):
    lane = lax.broadcasted_iota(jnp.int32, shape, 1)
    return jnp.where(lane < count, lane * per + quarter, -1)


def slot_split(shape, axis, first):
    slot = (lax.broadcasted_iota(jnp.int32, shape, axis) + first).astype(F32)
    lane = jnp.floor((slot + 0.5) * (1.0 / PAIR))
    rank = slot - PAIR * lane
    half = jnp.where(rank > CAP - 0.5, 1.0, 0.0)
    return lane, half, rank - CAP * half


def route_kernel(rows, per, count, q_ref, ids_ref, rw_ref, hid_ref, up_ref, gain_ref,
                 send_ref, st_ref, sw0_ref, sw1_ref, m_ref, r_ref, w_ref, n_ref):
    step = pl.program_id(0)
    tokens = ids_ref.shape[0]

    @pl.when(step == 0)
    def _():
        ids = ids_ref[...]
        weights = rw_ref[...].astype(F32)
        named = lane_expert(q_ref[0], per, count, (tokens, 128))
        member = jnp.zeros((tokens, 128), F32)
        weight = jnp.zeros((tokens, 128), F32)
        for k in range(ids.shape[1]):
            hit = ids[:, k : k + 1] == named
            member = member + jnp.where(hit, 1.0, 0.0)
            weight = weight + jnp.where(hit, weights[:, k : k + 1], 0.0)
        m_ref[...] = member.astype(BF)
        w_ref[...] = weight.astype(BF)
        row = lax.broadcasted_iota(jnp.int32, (tokens, tokens), 0)
        col = lax.broadcasted_iota(jnp.int32, (tokens, tokens), 1)
        below = jnp.where(col < row, 1.0, 0.0).astype(BF)
        r_ref[...] = nn(below, member.astype(BF)).astype(BF)
        wide = hid_ref[...].astype(F32)
        inv = lax.rsqrt(jnp.mean(wide * wide, axis=1, keepdims=True) + EPS)
        n_ref[:tokens] = (wide * inv * gain_ref[...]).astype(BF)
        n_ref[tokens:] = up_ref[...]

    first = step * rows
    member, rank, weight = m_ref[...], r_ref[...], w_ref[...]
    lane_of, half_of, rank_of = slot_split((rows, 128), 0, first)
    lane = lax.broadcasted_iota(jnp.int32, (rows, 128), 1).astype(F32)
    spread = jnp.where(lane == lane_of, 1.0, 0.0).astype(BF)
    chosen = (nt(spread, member) > 0.5) & (nt(spread, rank) == rank_of)
    s0 = jnp.where(chosen & (half_of < 0.5), 1.0, 0.0).astype(BF)
    s1 = jnp.where(chosen & (half_of > 0.5), 1.0, 0.0).astype(BF)
    send_ref[...] = nn(jnp.concatenate([s0, s1], axis=1), n_ref[...]).astype(BF)
    _, half_row, rank_row = slot_split((tokens, rows), 1, first)
    chosen_t = (nt(member, spread) > 0.5) & (nt(rank, spread) == rank_row)
    weight_t = nt(weight, spread)
    st_ref[...] = jnp.where(chosen_t & (half_row < 0.5), 1.0, 0.0).astype(BF)
    sw0_ref[...] = jnp.where(chosen_t & (half_row < 0.5), weight_t, 0.0).astype(BF)
    sw1_ref[...] = jnp.where(chosen_t & (half_row > 0.5), weight_t, 0.0).astype(BF)


def route(quarter, per, count, ids, weights, hidden, upstream, gain):
    tokens, width = hidden.shape
    rows = 384
    slots = count * PAIR
    matrix = pl.BlockSpec((tokens, rows), lambda i, p: (0, i))
    return pl.pallas_call(
        lambda *refs: route_kernel(rows, per, count, *refs),
        grid_spec=pltpu.PrefetchScalarGridSpec(
            num_scalar_prefetch=1,
            grid=(slots // rows,),
            in_specs=[
                whole((tokens, ids.shape[1])),
                whole((tokens, ids.shape[1])),
                whole((tokens, width)),
                whole((tokens, width)),
                whole((1, width)),
            ],
            out_specs=[pl.BlockSpec((rows, width), lambda i, p: (i, 0)), matrix, matrix, matrix],
            scratch_shapes=[
                pltpu.VMEM((tokens, 128), BF),
                pltpu.VMEM((tokens, 128), BF),
                pltpu.VMEM((tokens, 128), BF),
                pltpu.VMEM((2 * tokens, width), BF),
            ],
        ),
        out_shape=[jax.ShapeDtypeStruct((slots, width), BF)]
        + [jax.ShapeDtypeStruct((tokens, slots), BF)] * 3,
        compiler_params=params(),
        name="route",
    )(quarter, ids, weights, hidden, upstream, gain)


def expert_kernel(rows, q_ref, xy_ref, go_ref, uo_ref, do_ref, *refs):
    gu_refs, d_refs, out_ref = refs[:3], refs[3:6], refs[6]
    half_width = xy_ref.shape[1] // 2
    xy = xy_ref[...]
    w_gate = jnp.concatenate([go_ref[0]] + [r[0] for r in gu_refs], axis=1)
    w_up = jnp.concatenate([uo_ref[0]] + [r[1] for r in gu_refs], axis=1)
    w_down = jnp.concatenate([do_ref[0]] + [r[0] for r in d_refs], axis=0)
    gate = nn(xy, w_gate)
    up = nn(xy, w_up)
    proj = pltpu.roll(nt(xy, w_down), rows - CAP, 0)
    sig = 1.0 / (1.0 + jnp.exp(-gate))
    silu = gate * sig
    act = (silu * up).astype(BF).astype(F32)
    d_gate = (proj * up * (sig * (1.0 + gate * (1.0 - sig)))).astype(BF)
    d_up = (proj * silu).astype(BF)
    d_route = jnp.sum(act * proj, axis=1, keepdims=True)
    d_rows = nt(jnp.concatenate([d_gate, d_up], axis=1), jnp.concatenate([w_gate, w_up], axis=1))
    _, half, _ = slot_split((rows, 1), 0, 0)
    out = jnp.where(half > 0.5, pltpu.roll(d_rows[:, half_width:], CAP, 0), d_rows[:, :half_width])
    out_ref[:, :half_width] = out.astype(BF)
    out_ref[:, half_width:] = jnp.broadcast_to(d_route, (rows, 128)).astype(BF)


def expert(quarter, xy, w_gate, w_up, w_down, got_in, got_down):
    slots, width = xy.shape
    unit = w_gate.shape[2]
    rows = 384
    own = pl.BlockSpec((1, width, unit), lambda i, p: (p[0], 0, 0))
    return pl.pallas_call(
        lambda *refs: expert_kernel(rows, *refs),
        grid_spec=pltpu.PrefetchScalarGridSpec(
            num_scalar_prefetch=1,
            grid=(slots // rows,),
            in_specs=[
                pl.BlockSpec((rows, width), lambda i, p: (i, 0)),
                own,
                own,
                pl.BlockSpec((1, unit, width), lambda i, p: (p[0], 0, 0)),
            ]
            + [whole((2, width, unit))] * 3
            + [whole((1, unit, width))] * 3,
            out_specs=pl.BlockSpec((rows, width // 2 + 128), lambda i, p: (i, 0)),
        ),
        out_shape=jax.ShapeDtypeStruct((slots, width // 2 + 128), BF),
        compiler_params=params(),
        name="expert",
    )(quarter, xy, w_gate, w_up, w_down, *got_in, *got_down)


def gather_kernel(per, count, q_ref, back_ref, st_ref, sw0_ref, sw1_ref, ids_ref, hid_ref, gain_ref, out_ref):
    tokens, width = hid_ref.shape
    half_width = width // 2
    wide = hid_ref[...].astype(F32)
    inv = lax.rsqrt(jnp.mean(wide * wide, axis=1, keepdims=True) + EPS)
    rows = back_ref[:, :half_width]
    d_normed = jnp.concatenate([nn(sw0_ref[...], rows), nn(sw1_ref[...], rows)], axis=1)
    g = d_normed * gain_ref[...]
    inner = jnp.mean(g * wide, axis=1, keepdims=True)
    out_ref[:, :width] = (inv * g - wide * (inv * inv * inv * inner)).astype(BF)
    slots = back_ref.shape[0]
    lane_of, _, _ = slot_split((slots, 128), 0, 0)
    lane = lax.broadcasted_iota(jnp.int32, (slots, 128), 1).astype(F32)
    placed = jnp.where(lane == lane_of, back_ref[:, half_width:].astype(F32), 0.0).astype(BF)
    route = nn(st_ref[...], placed)
    named = lane_expert(q_ref[0], per, count, (tokens, 128))
    ids = ids_ref[...]
    column = lax.broadcasted_iota(jnp.int32, (tokens, 128), 1)
    out = jnp.zeros((tokens, 128), F32)
    for k in range(ids.shape[1]):
        value = jnp.sum(jnp.where(ids[:, k : k + 1] == named, route, 0.0), axis=1, keepdims=True)
        out = jnp.where(column == k, value, out)
    out_ref[:, width:] = out.astype(BF)


def on_chip(kernel, name, out_shape, scalars, arrays, scratch=()):
    vmem = pl.BlockSpec(memory_space=pltpu.VMEM)
    many = isinstance(out_shape, list)
    return pl.pallas_call(
        kernel,
        in_specs=[pl.BlockSpec(memory_space=pltpu.SMEM)] * len(scalars) + [vmem] * len(arrays),
        out_specs=[vmem] * len(out_shape) if many else vmem,
        out_shape=out_shape,
        scratch_shapes=list(scratch),
        compiler_params=params(),
        name=name,
    )(*scalars, *arrays)


def sum_first(ref):
    total = ref[0].astype(F32)
    for n in range(1, ref.shape[0]):
        total = total + ref[n].astype(F32)
    return total


def finish_kernel(z_ref, in_ref, up_ref, out_ref):
    parts, share, _ = in_ref.shape
    width = up_ref.shape[1]
    total = sum_first(in_ref)
    mine = up_ref[pl.ds(pl.multiple_of(z_ref[0] * share, share), share), :].astype(F32)
    done = jnp.concatenate([total[:, :width] + mine, total[:, width:]], axis=1).astype(BF)
    for n in range(parts):
        out_ref[n] = done


def add_kernel(a_ref, b_ref, out_ref):
    out_ref[...] = (a_ref[...].astype(F32) + b_ref[...].astype(F32)).astype(BF)


def spread_kernel(in_ref, out_ref):
    total = sum_first(in_ref).astype(BF)
    for n in range(out_ref.shape[0]):
        out_ref[n] = total


def last_kernel(in_ref, dk_ref, dv_ref):
    half = in_ref.shape[0] // 2
    for head in range(2):
        total = in_ref[head * half].astype(F32)
        for n in range(1, half):
            total = total + in_ref[head * half + n].astype(F32)
        at = slice(head * HEAD_DIM, (head + 1) * HEAD_DIM)
        dk_ref[:, at] = total[:, :HEAD_DIM]
        dv_ref[:, at] = total[:, HEAD_DIM:]


def heads_to_rows(x):
    return jnp.concatenate([x[:, :HEAD_DIM], x[:, HEAD_DIM:]], axis=0)


def probs_kernel(chunk, q_ref, a_ref, b_ref, p_ref, s_ref):
    half = a_ref.shape[0]
    query = heads_to_rows(q_ref[...])
    top = None
    for n in range(2 * half // chunk):
        src = a_ref if n * chunk < half else b_ref
        at = n * chunk % half
        s = nt(src[at : at + chunk, :HEAD_DIM], query) * SCALE
        s_ref[n * chunk : (n + 1) * chunk] = s
        most = jnp.max(s, axis=0, keepdims=True)
        top = most if top is None else jnp.maximum(top, most)
    total = jnp.zeros_like(top)
    for n in range(2 * half // chunk):
        e = jnp.exp(s_ref[n * chunk : (n + 1) * chunk] - top)
        s_ref[n * chunk : (n + 1) * chunk] = e
        total = total + jnp.sum(e, axis=0, keepdims=True)
    scale = 1.0 / total
    for n in range(2 * half // chunk):
        p_ref[n * chunk : (n + 1) * chunk] = (s_ref[n * chunk : (n + 1) * chunk] * scale).astype(BF)


def probs(queries, kv_a, kv_b):
    count = kv_a.shape[0] + kv_b.shape[0]
    rows = queries.shape[0] * 2
    return pl.pallas_call(
        lambda *refs: probs_kernel(512, *refs),
        out_shape=jax.ShapeDtypeStruct((count, rows), BF),
        scratch_shapes=[pltpu.VMEM((count, rows), F32)],
        compiler_params=params(),
        name="attention_probs",
    )(queries, kv_a, kv_b)


def grads_kernel(chunk, dh_ref, w_ref, q_ref, p_ref, a_ref, b_ref, dq_ref, da_ref, db_ref, dp_ref):
    half = a_ref.shape[0]
    width = w_ref.shape[1]
    d_out_w = nt(w_ref[...], dh_ref[:, :width]).astype(BF)
    d_one, d_two = d_out_w[:HEAD_DIM], d_out_w[HEAD_DIM:]
    d_out_t = jnp.concatenate([d_one, d_two], axis=1)
    d_out = jnp.concatenate([d_one.T, d_two.T], axis=0)
    query = heads_to_rows(q_ref[...])
    delta = jnp.zeros((1, d_out.shape[0]), F32)
    steps = 2 * half // chunk
    for n in range(steps):
        src = a_ref if n * chunk < half else b_ref
        at = n * chunk % half
        span = slice(n * chunk, (n + 1) * chunk)
        dp = nn(src[at : at + chunk, HEAD_DIM:], d_out_t)
        dp_ref[span] = dp
        delta = delta + jnp.sum(dp * p_ref[span].astype(F32), axis=0, keepdims=True)
    d_query = jnp.zeros((HEAD_DIM, d_out.shape[0]), F32)
    for n in range(steps):
        src, dst = (a_ref, da_ref) if n * chunk < half else (b_ref, db_ref)
        at = n * chunk % half
        span = slice(n * chunk, (n + 1) * chunk)
        p = p_ref[span]
        ds = (p.astype(F32) * (dp_ref[span] - delta)).astype(BF)
        dst[at : at + chunk, :HEAD_DIM] = (nn(ds, query) * SCALE).astype(BF)
        dst[at : at + chunk, HEAD_DIM:] = nn(p, d_out).astype(BF)
        d_query = d_query + tn(src[at : at + chunk, :HEAD_DIM], ds)
    d_query = (d_query * SCALE).T
    rows = q_ref.shape[0]
    dq_ref[:, :HEAD_DIM] = d_query[:rows]
    dq_ref[:, HEAD_DIM:] = d_query[rows:]


def body(hidden, upstream, norm_gain, route_ids, route_weights, w_gate, w_up, w_down, w_out, queries, keys, values):
    ctx_count = lax.axis_size("context")
    exp_count = lax.axis_size("expert")
    tokens, width = hidden.shape
    chips = ctx_count // 2
    per = w_gate.shape[0]
    slots = ctx_count * PAIR
    z = lax.axis_index("expert")
    quarter = z % per
    q_arr = quarter.astype(jnp.int32).reshape(1)
    z_arr = z.astype(jnp.int32).reshape(1)
    gain = norm_gain.reshape(1, width)
    swap_core = [(i, i ^ 1) for i in range(ctx_count)]
    same_core = [[2 * i + k for i in range(chips)] for k in range(2)]

    def far(core):
        return -2 if core == 0 else 2

    def moves(step):
        return [
            (i * ctx_count + c, (i + step(c % 2)) % exp_count * ctx_count + c)
            for c in range(ctx_count)
            for i in range(exp_count)
        ]

    got_in, got_down = [], []
    for shift, step in ((1, lambda core: 1), (per - 1, lambda core: -1), (2, far)):
        which = (z + shift) % per
        pick = [lax.dynamic_slice_in_dim(w, which, 1, 0) for w in (w_gate, w_up, w_down)]
        pair = moves(step)
        got_in.append(lax.ppermute(jnp.concatenate(pick[:2], axis=0), ("expert", "context"), pair))
        got_down.append(lax.ppermute(pick[2], ("expert", "context"), pair))

    kv_head = z // (exp_count // 2)
    own_kv = jnp.concatenate(
        [lax.dynamic_slice_in_dim(a, kv_head * HEAD_DIM, HEAD_DIM, 1) for a in (keys, values)], axis=1)
    kv_a = lax.all_gather(own_kv, "context", axis=0, tiled=True, axis_index_groups=same_core)

    send, st, sw0, sw1 = route(q_arr, per, ctx_count, route_ids, route_weights, hidden, upstream, gain)
    xy = lax.all_to_all(send.reshape(ctx_count, PAIR, width), "context", 0, 0, tiled=True)
    rows = expert(q_arr, xy.reshape(slots, width), w_gate, w_up, w_down, got_in, got_down)
    narrow = width // 2 + 128
    rows, kv_a = lax.optimization_barrier((rows, kv_a))
    rows = lax.all_to_all(rows.reshape(ctx_count, PAIR, narrow), "context", 0, 0, tiled=True)
    wide = width + 128
    q = on_chip(
        lambda *refs: gather_kernel(per, ctx_count, *refs), "gather_rows",
        jax.ShapeDtypeStruct((tokens, wide), BF),
        [q_arr], [rows.reshape(slots, narrow), st, sw0, sw1, route_ids, hidden, gain])

    share = tokens // exp_count
    parts = (exp_count, share, wide)
    arrived = lax.all_to_all(q.reshape(parts), "expert", 0, 0, tiled=True)
    done = on_chip(finish_kernel, "finish_hidden", jax.ShapeDtypeStruct(parts, BF), [z_arr], [arrived, upstream])
    done = lax.all_to_all(done, "expert", 0, 0, tiled=True).reshape(tokens, wide)
    d_hidden = done[:, :width]
    d_route = done[:, width : width + route_ids.shape[1]].astype(F32)

    kv_b = lax.ppermute(kv_a, "context", swap_core)
    queries, q = lax.optimization_barrier((queries, q))
    soft = probs(queries, kv_a, kv_b)
    d_queries, da, db = on_chip(
        lambda *refs: grads_kernel(512, *refs), "attention_grads",
        [
            jax.ShapeDtypeStruct(queries.shape, F32),
            jax.ShapeDtypeStruct(kv_a.shape, BF),
            jax.ShapeDtypeStruct(kv_b.shape, BF),
        ],
        [], [done, w_out, queries, soft, kv_a, kv_b], [pltpu.VMEM(soft.shape, F32)])
    db = lax.ppermute(db, "context", swap_core)
    part = on_chip(add_kernel, "add_cores", jax.ShapeDtypeStruct(da.shape, BF), [], [da, db])
    part = lax.all_to_all(
        part.reshape(chips, tokens, 2 * HEAD_DIM), "context", 0, 0, tiled=True, axis_index_groups=same_core)
    block = (exp_count, tokens, 2 * HEAD_DIM)
    part = on_chip(spread_kernel, "sum_chips", jax.ShapeDtypeStruct(block, BF), [], [part])
    part = lax.all_to_all(part, "expert", 0, 0, tiled=True)
    d_keys, d_values = on_chip(
        last_kernel, "sum_heads", [jax.ShapeDtypeStruct((tokens, 2 * HEAD_DIM), F32)] * 2, [], [part])
    return (d_hidden, d_route, d_queries, d_keys, d_values)


def solution(mesh):
    placed = (
        P("context", None),
        P("context", None),
        P(),
        P("context", None),
        P("context", None),
        P("context", None, "expert"),
        P("context", None, "expert"),
        P("context", "expert", None),
        P("expert", None),
        P("context", "expert"),
        P("context", None),
        P("context", None),
    )
    return jax.shard_map(
        body,
        mesh=mesh,
        in_specs=placed,
        out_specs=(
            P("context", None),
            P("context", None),
            P("context", "expert"),
            P("context", None),
            P("context", None),
        ),
        check_vma=False,
    )
```

```python
import math

import jax
import jax.numpy as jnp
from jax import lax
from jax.experimental import pallas as pl
from jax.experimental.pallas import tpu as pltpu
from jax.sharding import PartitionSpec as P

HEAD_DIM = 128
CAP = 12
PAIR = 2 * CAP
EPS = 1e-06
BF = jnp.bfloat16
F32 = jnp.float32
SCALE = 1.0 / math.sqrt(HEAD_DIM)
NT = (((1,), (1,)), ((), ()))
TN = (((0,), (0,)), ((), ()))
MB = 1 << 20
NEAR_MIB = 57
GRADS_MIB = 62
FINISH_MIB = 62
FAR_MIB = 60


def nt(a, b):
    return lax.dot_general(a, b, NT, preferred_element_type=F32)


def tn(a, b):
    return lax.dot_general(a, b, TN, preferred_element_type=F32)


def nn(a, b):
    return jnp.dot(a, b, preferred_element_type=F32)


def params(mib=60):
    return pltpu.CompilerParams(vmem_limit_bytes=mib * MB)


def whole(shape):
    return pl.BlockSpec(shape, lambda *_: (0,) * len(shape))


def row_expert(quarter, per, count, shape):
    row = lax.broadcasted_iota(jnp.int32, shape, 0)
    return jnp.where(row < count, row * per + quarter, -1)


def slot_split(shape, axis, first):
    slot = (lax.broadcasted_iota(jnp.int32, shape, axis) + first).astype(F32)
    lane = jnp.floor((slot + 0.5) * (1.0 / PAIR))
    rank = slot - PAIR * lane
    half = jnp.where(rank > CAP - 0.5, 1.0, 0.0)
    return lane, half, rank - CAP * half


def route_kernel(rows, per, count, q_ref, ids_ref, rw_ref, hid_ref, up_ref, gain_ref,
                 send_ref, s0_ref, sw0_ref, sw1_ref, m_ref, r_ref, w_ref, n_ref):
    step = pl.program_id(0)
    tokens = ids_ref.shape[1]

    @pl.when(step == 0)
    def _():
        ids = ids_ref[...]
        weights = rw_ref[...].astype(F32)
        named = row_expert(q_ref[0], per, count, (128, tokens))
        member = jnp.zeros((128, tokens), F32)
        weight = jnp.zeros((128, tokens), F32)
        for k in range(ids.shape[0]):
            hit = ids[k : k + 1] == named
            member = member + jnp.where(hit, 1.0, 0.0)
            weight = weight + jnp.where(hit, weights[k : k + 1], 0.0)
        m_ref[...] = member.astype(BF)
        w_ref[...] = weight.astype(BF)
        row = lax.broadcasted_iota(jnp.int32, (tokens, tokens), 0)
        col = lax.broadcasted_iota(jnp.int32, (tokens, tokens), 1)
        before = jnp.where(row < col, 1.0, 0.0).astype(BF)
        r_ref[...] = nn(member.astype(BF), before).astype(BF)
        wide = hid_ref[...].astype(F32)
        inv = lax.rsqrt(jnp.mean(wide * wide, axis=1, keepdims=True) + EPS)
        n_ref[:tokens] = (wide * inv * gain_ref[...]).astype(BF)
        n_ref[tokens:] = up_ref[...]

    lane_of, half_of, rank_of = slot_split((rows, 128), 0, step * rows)
    lane = lax.broadcasted_iota(jnp.int32, (rows, 128), 1).astype(F32)
    spread = jnp.where(lane == lane_of, 1.0, 0.0).astype(BF)
    chosen = (nn(spread, m_ref[...]) > 0.5) & (nn(spread, r_ref[...]) == rank_of)
    weight = nn(spread, w_ref[...])
    first, second = chosen & (half_of < 0.5), chosen & (half_of > 0.5)
    s0 = jnp.where(first, 1.0, 0.0).astype(BF)
    s1 = jnp.where(second, 1.0, 0.0).astype(BF)
    send_ref[...] = nn(jnp.concatenate([s0, s1], axis=1), n_ref[...]).astype(BF)
    s0_ref[...] = s0
    sw0_ref[...] = jnp.where(first, weight, 0.0).astype(BF)
    sw1_ref[...] = jnp.where(second, weight, 0.0).astype(BF)


def route(quarter, per, count, ids, weights, hidden, upstream, gain):
    tokens, width = hidden.shape
    rows = 256
    slots = count * PAIR
    matrix = pl.BlockSpec((rows, tokens), lambda i, p: (i, 0))
    return pl.pallas_call(
        lambda *refs: route_kernel(rows, per, count, *refs),
        grid_spec=pltpu.PrefetchScalarGridSpec(
            num_scalar_prefetch=1,
            grid=(slots // rows,),
            in_specs=[
                whole(ids.shape),
                whole(ids.shape),
                whole((tokens, width)),
                whole((tokens, width)),
                whole((1, width)),
            ],
            out_specs=[pl.BlockSpec((rows, width), lambda i, p: (i, 0)), matrix, matrix, matrix],
            scratch_shapes=[
                pltpu.VMEM((128, tokens), BF),
                pltpu.VMEM((128, tokens), BF),
                pltpu.VMEM((128, tokens), BF),
                pltpu.VMEM((2 * tokens, width), BF),
            ],
        ),
        out_shape=[jax.ShapeDtypeStruct((slots, width), BF)]
        + [jax.ShapeDtypeStruct((slots, tokens), BF)] * 3,
        compiler_params=params(),
        name="route",
    )(quarter, ids, weights, hidden, upstream, gain)


def pack_kernel(count, q_ref, g_ref, u_ref, d_ref, *refs):
    out_refs, sems = refs[:count], refs[count]
    unit = g_ref.shape[2]
    blocks = d_ref.shape[2] // unit
    copies = []
    for n, out in enumerate(out_refs):
        which = q_ref[n]
        pairs = [(g_ref.at[which], out.at[0]), (u_ref.at[which], out.at[1])]
        for k in range(blocks):
            at = pl.ds(k * unit, unit)
            pairs.append((d_ref.at[which, :, at], out.at[2, at]))
        copies += pairs
    copies = [pltpu.make_async_copy(src, dst, sems.at[k]) for k, (src, dst) in enumerate(copies)]
    for copy in copies:
        copy.start()
    for copy in copies:
        copy.wait()


def pack(which, w_gate, w_up, w_down):
    width, unit = w_gate.shape[1:]
    count = which.shape[0]
    hbm = pl.BlockSpec(memory_space=pltpu.HBM)
    return pl.pallas_call(
        lambda *refs: pack_kernel(count, *refs),
        in_specs=[pl.BlockSpec(memory_space=pltpu.SMEM), hbm, hbm, hbm],
        out_specs=[hbm] * count,
        out_shape=[jax.ShapeDtypeStruct((3, width, unit), BF)] * count,
        scratch_shapes=[pltpu.SemaphoreType.DMA((count * (2 + width // unit),))],
        compiler_params=params(),
        name="pack",
    )(which, w_gate, w_up, w_down)


def unpack(ref):
    unit = ref.shape[2]
    down = [ref[2, n * unit : (n + 1) * unit] for n in range(ref.shape[1] // unit)]
    return ref[0], ref[1], jnp.concatenate(down, axis=1)


def expert_rows(xy, w_in, w_down):
    rows, width = xy.shape
    half_width = width // 2
    ahead = nn(xy, w_in)
    gate, up = ahead[:, : w_in.shape[1] // 2], ahead[:, w_in.shape[1] // 2 :]
    proj = pltpu.roll(nt(xy, w_down), rows - CAP, 0)
    sig = 1.0 / (1.0 + jnp.exp(-gate))
    silu = gate * sig
    act = (silu * up).astype(BF).astype(F32)
    d_gate = (proj * up * (sig * (1.0 + gate * (1.0 - sig)))).astype(BF)
    d_up = (proj * silu).astype(BF)
    d_route = jnp.sum(act * proj, axis=1, keepdims=True)
    d_rows = nt(jnp.concatenate([d_gate, d_up], axis=1), w_in)
    _, half, _ = slot_split((rows, 1), 0, 0)
    out = jnp.where(half > 0.5, pltpu.roll(d_rows[:, half_width:], CAP, 0), d_rows[:, :half_width])
    return out, jnp.broadcast_to(d_route, (rows, 128))


def near_kernel(rows, q_ref, xy_ref, go_ref, uo_ref, do_ref, a_ref, b_ref, out_ref):
    width = xy_ref.shape[1]
    one, two = unpack(a_ref), unpack(b_ref)
    w_in = jnp.concatenate([go_ref[0], one[0], two[0], uo_ref[0], one[1], two[1]], axis=1)
    w_down = jnp.concatenate([do_ref[0], one[2], two[2]], axis=0)
    out, d_route = expert_rows(xy_ref[...], w_in, w_down)
    out_ref[:, : width // 2] = out
    out_ref[:, width // 2 :] = d_route


def expert_near(quarter, xy, w_gate, w_up, w_down, got_a, got_b):
    slots, width = xy.shape
    unit = w_gate.shape[2]
    rows = 384
    own = pl.BlockSpec((1, width, unit), lambda i, p: (p[0], 0, 0))
    narrow = width // 2 + 128
    return pl.pallas_call(
        lambda *refs: near_kernel(rows, *refs),
        grid_spec=pltpu.PrefetchScalarGridSpec(
            num_scalar_prefetch=1,
            grid=(slots // rows,),
            in_specs=[
                pl.BlockSpec((rows, width), lambda i, p: (i, 0)),
                own,
                own,
                pl.BlockSpec((1, unit, width), lambda i, p: (p[0], 0, 0)),
                whole(got_a.shape),
                whole(got_b.shape),
            ],
            out_specs=pl.BlockSpec((rows, narrow), lambda i, p: (i, 0)),
        ),
        out_shape=jax.ShapeDtypeStruct((slots, narrow), F32),
        compiler_params=params(NEAR_MIB),
        name="expert_near",
    )(quarter, xy, w_gate, w_up, w_down, got_a, got_b)


def far_kernel(xy_ref, far_ref, near_ref, out_ref):
    width = xy_ref.shape[1]
    w_gate, w_up, w_down = unpack(far_ref)
    out, d_route = expert_rows(xy_ref[...], jnp.concatenate([w_gate, w_up], axis=1), w_down)
    out_ref[:, : width // 2] = (near_ref[:, : width // 2] + out).astype(BF)
    out_ref[:, width // 2 :] = (near_ref[:, width // 2 :] + d_route).astype(BF)


def expert_far(xy, got, near):
    slots, width = xy.shape
    narrow = near.shape[1]
    rows = 192
    block = pl.BlockSpec((rows, narrow), lambda i: (i, 0))
    return pl.pallas_call(
        far_kernel,
        grid=(slots // rows,),
        in_specs=[pl.BlockSpec((rows, width), lambda i: (i, 0)), whole(got.shape), block],
        out_specs=block,
        out_shape=jax.ShapeDtypeStruct((slots, narrow), BF),
        compiler_params=params(FAR_MIB),
        name="expert_far",
    )(xy, got, near)


def gather_kernel(per, count, q_ref, back_ref, s0_ref, sw0_ref, sw1_ref, ids_ref, hid_ref, gain_ref, out_ref):
    tokens, width = hid_ref.shape
    half_width = width // 2
    wide = hid_ref[...].astype(F32)
    inv = lax.rsqrt(jnp.mean(wide * wide, axis=1, keepdims=True) + EPS)
    rows = back_ref[:, :half_width]
    d_normed = jnp.concatenate([tn(sw0_ref[...], rows), tn(sw1_ref[...], rows)], axis=1)
    g = d_normed * gain_ref[...]
    inner = jnp.mean(g * wide, axis=1, keepdims=True)
    out_ref[:, :width] = (inv * g - wide * (inv * inv * inv * inner)).astype(BF)
    slots = back_ref.shape[0]
    lane_of, _, _ = slot_split((slots, 128), 0, 0)
    lane = lax.broadcasted_iota(jnp.int32, (slots, 128), 1).astype(F32)
    placed = jnp.where(lane == lane_of, back_ref[:, half_width:].astype(F32), 0.0).astype(BF)
    route = tn(placed, s0_ref[...])
    named = row_expert(q_ref[0], per, count, (128, tokens))
    ids = ids_ref[...]
    row = lax.broadcasted_iota(jnp.int32, (128, tokens), 0)
    out = jnp.zeros((128, tokens), F32)
    for k in range(ids.shape[0]):
        value = jnp.sum(jnp.where(ids[k : k + 1] == named, route, 0.0), axis=0, keepdims=True)
        out = jnp.where(row == k, value, out)
    out_ref[:, width:] = out.T.astype(BF)


def on_chip(kernel, name, out_shape, scalars, arrays, scratch=(), mib=60):
    vmem = pl.BlockSpec(memory_space=pltpu.VMEM)
    many = isinstance(out_shape, list)
    return pl.pallas_call(
        kernel,
        in_specs=[pl.BlockSpec(memory_space=pltpu.SMEM)] * len(scalars) + [vmem] * len(arrays),
        out_specs=[vmem] * len(out_shape) if many else vmem,
        out_shape=out_shape,
        scratch_shapes=list(scratch),
        compiler_params=params(mib),
        name=name,
    )(*scalars, *arrays)


def sum_first(ref):
    total = ref[0].astype(F32)
    for n in range(1, ref.shape[0]):
        total = total + ref[n].astype(F32)
    return total


def finish_kernel(z_ref, in_ref, up_ref, out_ref):
    width = up_ref.shape[1]
    total = sum_first(in_ref)
    mine = up_ref[...].astype(F32)
    done = jnp.concatenate([total[:, :width] + mine, total[:, width:]], axis=1).astype(BF)
    for n in range(in_ref.shape[0]):
        out_ref[n] = done


def finish(z, arrived, upstream):
    parts, share, wide = arrived.shape
    return pl.pallas_call(
        finish_kernel,
        grid_spec=pltpu.PrefetchScalarGridSpec(
            num_scalar_prefetch=1,
            grid=(1,),
            in_specs=[
                whole((parts, share, wide)),
                pl.BlockSpec((share, upstream.shape[1]), lambda i, z: (z[0], 0)),
            ],
            out_specs=whole((parts, share, wide)),
        ),
        out_shape=jax.ShapeDtypeStruct((parts, share, wide), BF),
        compiler_params=params(FINISH_MIB),
        name="finish_hidden",
    )(z, arrived, upstream)


def spread_kernel(in_ref, out_ref):
    total = sum_first(in_ref).astype(BF)
    for n in range(out_ref.shape[0]):
        out_ref[n] = total


def last_kernel(in_ref, dk_ref, dv_ref):
    half = in_ref.shape[0] // 2
    for head in range(2):
        total = in_ref[head * half].astype(F32)
        for n in range(1, half):
            total = total + in_ref[head * half + n].astype(F32)
        at = slice(head * HEAD_DIM, (head + 1) * HEAD_DIM)
        dk_ref[:, at] = total[:, :HEAD_DIM]
        dv_ref[:, at] = total[:, HEAD_DIM:]


def heads_to_rows(x):
    return jnp.concatenate([x[:, :HEAD_DIM], x[:, HEAD_DIM:]], axis=0)


def probs_kernel(chunk, q_ref, o_ref, kv_ref, p_ref, stat_ref, s_ref):
    query = jnp.concatenate([heads_to_rows(q_ref[...]), heads_to_rows(o_ref[...])], axis=0)
    count = query.shape[0]
    steps = [slice(n, n + chunk) for n in range(0, kv_ref.shape[0], chunk)]
    top = None
    for span in steps:
        s = nt(kv_ref[span, :HEAD_DIM], query) * SCALE
        s_ref[span] = s
        most = jnp.max(s, axis=0, keepdims=True)
        top = most if top is None else jnp.maximum(top, most)
    total = jnp.zeros_like(top)
    out = jnp.zeros((HEAD_DIM, count), F32)
    for span in steps:
        e = jnp.exp(s_ref[span] - top)
        total = total + jnp.sum(e, axis=0, keepdims=True)
        p = e.astype(BF)
        p_ref[span] = p
        out = out + tn(kv_ref[span, HEAD_DIM:], p)
    stat_ref[:HEAD_DIM] = out
    row = lax.broadcasted_iota(jnp.int32, (8, count), 0)
    stat_ref[HEAD_DIM:] = jnp.where(row == 0, top, total)


def probs(queries, other, kv):
    count = kv.shape[0]
    rows = queries.shape[0] * 4
    return on_chip(
        lambda *refs: probs_kernel(512, *refs), "attention_probs",
        [jax.ShapeDtypeStruct((count, rows), BF), jax.ShapeDtypeStruct((HEAD_DIM + 8, rows), F32)],
        [], [queries, other, kv], [pltpu.VMEM((count, rows), F32)])


def grads_kernel(chunk, dh_ref, do_ref, w_ref, q_ref, o_ref, p_ref, stat_ref, far_ref, kv_ref, dq_ref, dqo_ref, dkv_ref):
    width = w_ref.shape[1]
    tokens = dh_ref.shape[0]
    d_hidden = jnp.concatenate([dh_ref[:, :width], do_ref[:, :width]], axis=0)
    d_out_w = nt(w_ref[...], d_hidden).astype(BF)
    parts = [d_out_w[h * HEAD_DIM : (h + 1) * HEAD_DIM, c * tokens : (c + 1) * tokens] for c in range(2) for h in range(2)]
    d_out_t = jnp.concatenate(parts, axis=1)
    d_out = jnp.concatenate([p.T for p in parts], axis=0)
    query = jnp.concatenate([heads_to_rows(q_ref[...]), heads_to_rows(o_ref[...])], axis=0)
    half = query.shape[0] // 2
    here = stat_ref[...]
    there = jnp.concatenate([far_ref[:, half:], far_ref[:, :half]], axis=1)
    top_here, top_there = here[HEAD_DIM : HEAD_DIM + 1], there[HEAD_DIM : HEAD_DIM + 1]
    top = jnp.maximum(top_here, top_there)
    in_here, in_there = jnp.exp(top_here - top), jnp.exp(top_there - top)
    total = here[HEAD_DIM + 1 : HEAD_DIM + 2] * in_here + there[HEAD_DIM + 1 : HEAD_DIM + 2] * in_there
    in_here, in_there = in_here / total, in_there / total
    out = here[:HEAD_DIM] * in_here + there[:HEAD_DIM] * in_there
    delta = jnp.sum(d_out_t.astype(F32) * out, axis=0, keepdims=True)
    d_query = jnp.zeros((HEAD_DIM, 2 * half), F32)
    for n in range(0, kv_ref.shape[0], chunk):
        span = slice(n, n + chunk)
        p = p_ref[span].astype(F32) * in_here
        d_probs = nn(kv_ref[span, HEAD_DIM:], d_out_t)
        ds = (p * (d_probs - delta)).astype(BF)
        dkv_ref[span, :HEAD_DIM] = (nn(ds, query) * SCALE).astype(BF)
        dkv_ref[span, HEAD_DIM:] = nn(p.astype(BF), d_out).astype(BF)
        d_query = d_query + tn(kv_ref[span, :HEAD_DIM], ds)
    d_query = (d_query * SCALE).T
    for ref, at in ((dq_ref, 0), (dqo_ref, half)):
        ref[:, :HEAD_DIM] = d_query[at : at + tokens]
        ref[:, HEAD_DIM:] = d_query[at + tokens : at + 2 * tokens]


def body(hidden, upstream, norm_gain, route_ids, route_weights, w_gate, w_up, w_down, w_out, queries, keys, values):
    ctx_count = lax.axis_size("context")
    exp_count = lax.axis_size("expert")
    tokens, width = hidden.shape
    chips = ctx_count // 2
    per = w_gate.shape[0]
    slots = ctx_count * PAIR
    z = lax.axis_index("expert")
    quarter = z % per
    q_arr = quarter.astype(jnp.int32).reshape(1)
    z_arr = z.astype(jnp.int32).reshape(1)
    gain = norm_gain.reshape(1, width)
    swap_core = [(i, i ^ 1) for i in range(ctx_count)]
    same_core = [[2 * i + k for i in range(chips)] for k in range(2)]

    def far(core):
        return -2 if core == 0 else 2

    def moves(step):
        return [
            (i * ctx_count + c, (i + step(c % 2)) % exp_count * ctx_count + c)
            for c in range(ctx_count)
            for i in range(exp_count)
        ]

    def trade(w, step):
        return lax.ppermute(w, ("expert", "context"), moves(step))

    leave = [((z + n) % per).astype(jnp.int32) for n in (1, per - 1, 2)]
    packs = pack(jnp.stack(leave[:2]), w_gate, w_up, w_down) + pack(jnp.stack(leave[2:]), w_gate, w_up, w_down)
    near_a, near_b = trade(packs[0], lambda core: 1), trade(packs[1], lambda core: -1)
    distant, near_a, near_b = lax.optimization_barrier((packs[2], near_a, near_b))
    got_far = trade(distant, far)

    ids = route_ids.T
    kv_head = z // (exp_count // 2)
    own_kv = jnp.concatenate(
        [lax.dynamic_slice_in_dim(a, kv_head * HEAD_DIM, HEAD_DIM, 1) for a in (keys, values)], axis=1)
    kv = lax.all_gather(own_kv, "context", axis=0, tiled=True, axis_index_groups=same_core)

    send, s0, sw0, sw1 = route(q_arr, per, ctx_count, ids, route_weights.T, hidden, upstream, gain)
    xy = lax.all_to_all(send.reshape(ctx_count, PAIR, width), "context", 0, 0, tiled=True)
    xy = xy.reshape(slots, width)
    narrow = width // 2 + 128
    near = expert_near(q_arr, xy, w_gate, w_up, w_down, near_a, near_b)
    rows = expert_far(xy, got_far, near)
    rows, kv = lax.optimization_barrier((rows, kv))
    rows = lax.all_to_all(rows.reshape(ctx_count, PAIR, narrow), "context", 0, 0, tiled=True)
    wide = width + 128
    q = on_chip(
        lambda *refs: gather_kernel(per, ctx_count, *refs), "gather_rows",
        jax.ShapeDtypeStruct((tokens, wide), BF),
        [q_arr], [rows.reshape(slots, narrow), s0, sw0, sw1, ids, hidden, gain])

    share = tokens // exp_count
    parts = (exp_count, share, wide)
    arrived = lax.all_to_all(q.reshape(parts), "expert", 0, 0, tiled=True)
    queries, q = lax.optimization_barrier((queries, q))
    other = lax.ppermute(queries, "context", swap_core)
    soft, stats = probs(queries, other, kv)
    far_stats = lax.ppermute(stats, "context", swap_core)
    arrived, far_stats = lax.optimization_barrier((arrived, far_stats))
    done = finish(z_arr, arrived, upstream)
    done = lax.all_to_all(done, "expert", 0, 0, tiled=True).reshape(tokens, wide)
    d_hidden = done[:, :width]
    d_route = done[:, width : width + route_ids.shape[1]].astype(F32)

    done_other = lax.ppermute(done, "context", swap_core)
    d_queries, d_other, part = on_chip(
        lambda *refs: grads_kernel(512, *refs), "attention_grads",
        [
            jax.ShapeDtypeStruct(queries.shape, F32),
            jax.ShapeDtypeStruct(queries.shape, F32),
            jax.ShapeDtypeStruct(kv.shape, BF),
        ],
        [], [done, done_other, w_out, queries, other, soft, stats, far_stats, kv], mib=GRADS_MIB)
    d_queries = d_queries + lax.ppermute(d_other, "context", swap_core)
    part = lax.all_to_all(
        part.reshape(chips, tokens, 2 * HEAD_DIM), "context", 0, 0, tiled=True, axis_index_groups=same_core)
    block = (exp_count, tokens, 2 * HEAD_DIM)
    part = on_chip(spread_kernel, "sum_chips", jax.ShapeDtypeStruct(block, BF), [], [part], mib=32)
    part = lax.all_to_all(part, "expert", 0, 0, tiled=True)
    d_keys, d_values = on_chip(
        last_kernel, "sum_heads", [jax.ShapeDtypeStruct((tokens, 2 * HEAD_DIM), F32)] * 2, [], [part], mib=32)
    return (d_hidden, d_route, d_queries, d_keys, d_values)


def solution(mesh):
    placed = (
        P("context", None),
        P("context", None),
        P(),
        P("context", None),
        P("context", None),
        P("context", None, "expert"),
        P("context", None, "expert"),
        P("context", "expert", None),
        P("expert", None),
        P("context", "expert"),
        P("context", None),
        P("context", None),
    )
    return jax.shard_map(
        body,
        mesh=mesh,
        in_specs=placed,
        out_specs=(
            P("context", None),
            P("context", None),
            P("context", "expert"),
            P("context", None),
            P("context", None),
        ),
        check_vma=False,
    )
```

```python
import math

import jax
import jax.numpy as jnp
from jax import lax
from jax.experimental import pallas as pl
from jax.experimental.pallas import tpu as pltpu
from jax.sharding import PartitionSpec as P

HEAD_DIM = 128
CAP = 12
BF = jnp.bfloat16
F32 = jnp.float32
PAIR = 2 * CAP
EPS = 1e-06
SCALE = 1.0 / math.sqrt(HEAD_DIM)
NT = (((1,), (1,)), ((), ()))
TN = (((0,), (0,)), ((), ()))
MB = 1 << 20
NEAR_MIB = 60
PACK_ROWS = 1024
NEAR_TYPE = BF
NEAR_ROWS = 384
FAR_ROWS = 384
GRADS_MIB = 62
FINISH_MIB = 32
FAR_MIB = 60


def nt(a, b):
    return lax.dot_general(a, b, NT, preferred_element_type=F32)


def tn(a, b):
    return lax.dot_general(a, b, TN, preferred_element_type=F32)


def nn(a, b):
    return jnp.dot(a, b, preferred_element_type=F32)


def params(mib=60):
    return pltpu.CompilerParams(vmem_limit_bytes=mib * MB)


def whole(shape):
    return pl.BlockSpec(shape, lambda *_: (0,) * len(shape))


def row_expert(quarter, per, count, shape):
    row = lax.broadcasted_iota(jnp.int32, shape, 0)
    return jnp.where(row < count, row * per + quarter, -1)


def slot_split(shape, axis, first):
    slot = (lax.broadcasted_iota(jnp.int32, shape, axis) + first).astype(F32)
    lane = jnp.floor((slot + 0.5) * (1.0 / PAIR))
    rank = slot - PAIR * lane
    half = jnp.where(rank > CAP - 0.5, 1.0, 0.0)
    return lane, half, rank - CAP * half


def route_kernel(rows, per, count, q_ref, ids_ref, rw_ref, hid_ref, up_ref, gain_ref,
                 send_ref, s0_ref, sw0_ref, sw1_ref, m_ref, r_ref, w_ref, n_ref):
    step = pl.program_id(0)
    tokens = ids_ref.shape[1]

    @pl.when(step == 0)
    def _():
        ids = ids_ref[...]
        weights = rw_ref[...].astype(F32)
        named = row_expert(q_ref[0], per, count, (128, tokens))
        member = jnp.zeros((128, tokens), F32)
        weight = jnp.zeros((128, tokens), F32)
        for k in range(ids.shape[0]):
            hit = ids[k : k + 1] == named
            member = member + jnp.where(hit, 1.0, 0.0)
            weight = weight + jnp.where(hit, weights[k : k + 1], 0.0)
        m_ref[...] = member.astype(BF)
        w_ref[...] = weight.astype(BF)
        row = lax.broadcasted_iota(jnp.int32, (tokens, tokens), 0)
        col = lax.broadcasted_iota(jnp.int32, (tokens, tokens), 1)
        before = jnp.where(row < col, 1.0, 0.0).astype(BF)
        r_ref[...] = nn(member.astype(BF), before).astype(BF)
        wide = hid_ref[...].astype(F32)
        inv = lax.rsqrt(jnp.mean(wide * wide, axis=1, keepdims=True) + EPS)
        n_ref[:tokens] = (wide * inv * gain_ref[...]).astype(BF)
        n_ref[tokens:] = up_ref[...]

    lane_of, half_of, rank_of = slot_split((rows, 128), 0, step * rows)
    lane = lax.broadcasted_iota(jnp.int32, (rows, 128), 1).astype(F32)
    spread = jnp.where(lane == lane_of, 1.0, 0.0).astype(BF)
    chosen = (nn(spread, m_ref[...]) > 0.5) & (nn(spread, r_ref[...]) == rank_of)
    weight = nn(spread, w_ref[...])
    first, second = chosen & (half_of < 0.5), chosen & (half_of > 0.5)
    s0 = jnp.where(first, 1.0, 0.0).astype(BF)
    s1 = jnp.where(second, 1.0, 0.0).astype(BF)
    send_ref[...] = nn(jnp.concatenate([s0, s1], axis=1), n_ref[...]).astype(BF)
    s0_ref[...] = s0
    sw0_ref[...] = jnp.where(first, weight, 0.0).astype(BF)
    sw1_ref[...] = jnp.where(second, weight, 0.0).astype(BF)


def route(quarter, per, count, ids, weights, hidden, upstream, gain):
    tokens, width = hidden.shape
    rows = 256
    slots = count * PAIR
    matrix = pl.BlockSpec((rows, tokens), lambda i, p: (i, 0))
    return pl.pallas_call(
        lambda *refs: route_kernel(rows, per, count, *refs),
        grid_spec=pltpu.PrefetchScalarGridSpec(
            num_scalar_prefetch=1,
            grid=(slots // rows,),
            in_specs=[
                whole(ids.shape),
                whole(ids.shape),
                whole((tokens, width)),
                whole((tokens, width)),
                whole((1, width)),
            ],
            out_specs=[pl.BlockSpec((rows, width), lambda i, p: (i, 0)), matrix, matrix, matrix],
            scratch_shapes=[
                pltpu.VMEM((128, tokens), BF),
                pltpu.VMEM((128, tokens), BF),
                pltpu.VMEM((128, tokens), BF),
                pltpu.VMEM((2 * tokens, width), BF),
            ],
        ),
        out_shape=[jax.ShapeDtypeStruct((slots, width), BF)]
        + [jax.ShapeDtypeStruct((slots, tokens), BF)] * 3,
        compiler_params=params(),
        name="route",
    )(quarter, ids, weights, hidden, upstream, gain)


def pack_kernel(count, q_ref, *refs):
    for n in range(count):
        g_ref, u_ref, d_ref = refs[3 * n : 3 * n + 3]
        out_ref = refs[3 * count + n]
        unit = g_ref.shape[2]
        out_ref[0] = g_ref[0]
        out_ref[1] = u_ref[0]
        for k in range(d_ref.shape[2] // unit):
            out_ref[2, k * unit : (k + 1) * unit] = d_ref[0, :, k * unit : (k + 1) * unit]


def pack(which, w_gate, w_up, w_down):
    width, unit = w_gate.shape[1:]
    count = which.shape[0]
    rows = PACK_ROWS

    def at(n):
        tall = pl.BlockSpec((1, rows, unit), lambda i, q: (q[n], i, 0))
        return [tall, tall, pl.BlockSpec((1, unit, rows), lambda i, q: (q[n], 0, i))]

    return pl.pallas_call(
        lambda *refs: pack_kernel(count, *refs),
        grid_spec=pltpu.PrefetchScalarGridSpec(
            num_scalar_prefetch=1,
            grid=(width // rows,),
            in_specs=sum([at(n) for n in range(count)], []),
            out_specs=[pl.BlockSpec((3, rows, unit), lambda i, q: (0, i, 0))] * count,
        ),
        out_shape=[jax.ShapeDtypeStruct((3, width, unit), BF)] * count,
        compiler_params=params(),
        name="pack",
    )(which, *[w_gate, w_up, w_down] * count)


def unpack(ref):
    unit = ref.shape[2]
    down = [ref[2, n * unit : (n + 1) * unit] for n in range(ref.shape[1] // unit)]
    return ref[0], ref[1], jnp.concatenate(down, axis=1)


def expert_rows(xy, w_in, w_down):
    rows, width = xy.shape
    half_width = width // 2
    ahead = nn(xy, w_in)
    gate, up = ahead[:, : w_in.shape[1] // 2], ahead[:, w_in.shape[1] // 2 :]
    proj = pltpu.roll(nt(xy, w_down), rows - CAP, 0)
    sig = 1.0 / (1.0 + jnp.exp(-gate))
    silu = gate * sig
    act = (silu * up).astype(BF).astype(F32)
    d_gate = (proj * up * (sig * (1.0 + gate * (1.0 - sig)))).astype(BF)
    d_up = (proj * silu).astype(BF)
    d_route = jnp.sum(act * proj, axis=1, keepdims=True)
    d_rows = nt(jnp.concatenate([d_gate, d_up], axis=1), w_in)
    _, half, _ = slot_split((rows, 1), 0, 0)
    out = jnp.where(half > 0.5, pltpu.roll(d_rows[:, half_width:], CAP, 0), d_rows[:, :half_width])
    return out, jnp.broadcast_to(d_route, (rows, 128))


def near_kernel(rows, q_ref, xy_ref, go_ref, uo_ref, do_ref, a_ref, b_ref, out_ref):
    width = xy_ref.shape[1]
    one, two = unpack(a_ref), unpack(b_ref)
    w_in = jnp.concatenate([go_ref[0], one[0], two[0], uo_ref[0], one[1], two[1]], axis=1)
    w_down = jnp.concatenate([do_ref[0], one[2], two[2]], axis=0)
    out, d_route = expert_rows(xy_ref[...], w_in, w_down)
    out_ref[:, : width // 2] = out.astype(NEAR_TYPE)
    out_ref[:, width // 2 :] = d_route.astype(NEAR_TYPE)


def expert_near(quarter, xy, w_gate, w_up, w_down, got_a, got_b):
    slots, width = xy.shape
    unit = w_gate.shape[2]
    rows = NEAR_ROWS
    own = pl.BlockSpec((1, width, unit), lambda i, p: (p[0], 0, 0))
    narrow = width // 2 + 128
    return pl.pallas_call(
        lambda *refs: near_kernel(rows, *refs),
        grid_spec=pltpu.PrefetchScalarGridSpec(
            num_scalar_prefetch=1,
            grid=(slots // rows,),
            in_specs=[
                pl.BlockSpec((rows, width), lambda i, p: (i, 0)),
                own,
                own,
                pl.BlockSpec((1, unit, width), lambda i, p: (p[0], 0, 0)),
                whole(got_a.shape),
                whole(got_b.shape),
            ],
            out_specs=pl.BlockSpec((rows, narrow), lambda i, p: (i, 0)),
        ),
        out_shape=jax.ShapeDtypeStruct((slots, narrow), NEAR_TYPE),
        compiler_params=params(NEAR_MIB),
        name="expert_near",
    )(quarter, xy, w_gate, w_up, w_down, got_a, got_b)


def far_kernel(xy_ref, far_ref, near_ref, out_ref):
    width = xy_ref.shape[1]
    w_gate, w_up, w_down = unpack(far_ref)
    out, d_route = expert_rows(xy_ref[...], jnp.concatenate([w_gate, w_up], axis=1), w_down)
    out_ref[:, : width // 2] = (near_ref[:, : width // 2] + out).astype(BF)
    out_ref[:, width // 2 :] = (near_ref[:, width // 2 :] + d_route).astype(BF)


def expert_far(xy, got, near):
    slots, width = xy.shape
    narrow = near.shape[1]
    rows = FAR_ROWS
    block = pl.BlockSpec((rows, narrow), lambda i: (i, 0))
    return pl.pallas_call(
        far_kernel,
        grid=(slots // rows,),
        in_specs=[pl.BlockSpec((rows, width), lambda i: (i, 0)), whole(got.shape), block],
        out_specs=block,
        out_shape=jax.ShapeDtypeStruct((slots, narrow), BF),
        compiler_params=params(FAR_MIB),
        name="expert_far",
    )(xy, got, near)


def gather_kernel(per, count, q_ref, back_ref, s0_ref, sw0_ref, sw1_ref, ids_ref, hid_ref, gain_ref, out_ref):
    tokens, width = hid_ref.shape
    half_width = width // 2
    wide = hid_ref[...].astype(F32)
    inv = lax.rsqrt(jnp.mean(wide * wide, axis=1, keepdims=True) + EPS)
    rows = back_ref[:, :half_width]
    d_normed = jnp.concatenate([tn(sw0_ref[...], rows), tn(sw1_ref[...], rows)], axis=1)
    g = d_normed * gain_ref[...]
    inner = jnp.mean(g * wide, axis=1, keepdims=True)
    out_ref[:, :width] = (inv * g - wide * (inv * inv * inv * inner)).astype(BF)
    slots = back_ref.shape[0]
    lane_of, _, _ = slot_split((slots, 128), 0, 0)
    lane = lax.broadcasted_iota(jnp.int32, (slots, 128), 1).astype(F32)
    placed = jnp.where(lane == lane_of, back_ref[:, half_width:].astype(F32), 0.0).astype(BF)
    route = tn(placed, s0_ref[...])
    named = row_expert(q_ref[0], per, count, (128, tokens))
    ids = ids_ref[...]
    row = lax.broadcasted_iota(jnp.int32, (128, tokens), 0)
    out = jnp.zeros((128, tokens), F32)
    for k in range(ids.shape[0]):
        value = jnp.sum(jnp.where(ids[k : k + 1] == named, route, 0.0), axis=0, keepdims=True)
        out = jnp.where(row == k, value, out)
    out_ref[:, width:] = out.T.astype(BF)


def on_chip(kernel, name, out_shape, scalars, arrays, scratch=(), mib=60):
    vmem = pl.BlockSpec(memory_space=pltpu.VMEM)
    many = isinstance(out_shape, list)
    return pl.pallas_call(
        kernel,
        in_specs=[pl.BlockSpec(memory_space=pltpu.SMEM)] * len(scalars) + [vmem] * len(arrays),
        out_specs=[vmem] * len(out_shape) if many else vmem,
        out_shape=out_shape,
        scratch_shapes=list(scratch),
        compiler_params=params(mib),
        name=name,
    )(*scalars, *arrays)


def sum_first(ref):
    total = ref[0].astype(F32)
    for n in range(1, ref.shape[0]):
        total = total + ref[n].astype(F32)
    return total


def finish_kernel(z_ref, in_ref, up_ref, out_ref):
    width = up_ref.shape[1]
    total = sum_first(in_ref)
    mine = up_ref[...].astype(F32)
    done = jnp.concatenate([total[:, :width] + mine, total[:, width:]], axis=1).astype(BF)
    for n in range(in_ref.shape[0]):
        out_ref[n] = done


def finish(z, arrived, upstream):
    parts, share, wide = arrived.shape
    return pl.pallas_call(
        finish_kernel,
        grid_spec=pltpu.PrefetchScalarGridSpec(
            num_scalar_prefetch=1,
            grid=(1,),
            in_specs=[
                whole((parts, share, wide)),
                pl.BlockSpec((share, upstream.shape[1]), lambda i, z: (z[0], 0)),
            ],
            out_specs=whole((parts, share, wide)),
        ),
        out_shape=jax.ShapeDtypeStruct((parts, share, wide), BF),
        compiler_params=params(FINISH_MIB),
        name="finish_hidden",
    )(z, arrived, upstream)


def spread_kernel(in_ref, out_ref):
    total = sum_first(in_ref).astype(BF)
    for n in range(out_ref.shape[0]):
        out_ref[n] = total


def last_kernel(in_ref, dk_ref, dv_ref):
    half = in_ref.shape[0] // 2
    for head in range(2):
        total = in_ref[head * half].astype(F32)
        for n in range(1, half):
            total = total + in_ref[head * half + n].astype(F32)
        at = slice(head * HEAD_DIM, (head + 1) * HEAD_DIM)
        dk_ref[:, at] = total[:, :HEAD_DIM]
        dv_ref[:, at] = total[:, HEAD_DIM:]


def heads_to_rows(x):
    return jnp.concatenate([x[:, :HEAD_DIM], x[:, HEAD_DIM:]], axis=0)


def probs_kernel(chunk, q_ref, o_ref, kv_ref, p_ref, stat_ref, s_ref):
    query = jnp.concatenate([heads_to_rows(q_ref[...]), heads_to_rows(o_ref[...])], axis=0)
    count = query.shape[0]
    steps = [slice(n, n + chunk) for n in range(0, kv_ref.shape[0], chunk)]
    top = None
    for span in steps:
        s = nt(kv_ref[span, :HEAD_DIM], query) * SCALE
        s_ref[span] = s
        most = jnp.max(s, axis=0, keepdims=True)
        top = most if top is None else jnp.maximum(top, most)
    total = jnp.zeros_like(top)
    out = jnp.zeros((HEAD_DIM, count), F32)
    for span in steps:
        e = jnp.exp(s_ref[span] - top)
        total = total + jnp.sum(e, axis=0, keepdims=True)
        p = e.astype(BF)
        p_ref[span] = p
        out = out + tn(kv_ref[span, HEAD_DIM:], p)
    stat_ref[:HEAD_DIM] = out
    row = lax.broadcasted_iota(jnp.int32, (8, count), 0)
    stat_ref[HEAD_DIM:] = jnp.where(row == 0, top, total)


def probs(queries, other, kv):
    count = kv.shape[0]
    rows = queries.shape[0] * 4
    return on_chip(
        lambda *refs: probs_kernel(512, *refs), "attention_probs",
        [jax.ShapeDtypeStruct((count, rows), BF), jax.ShapeDtypeStruct((HEAD_DIM + 8, rows), F32)],
        [], [queries, other, kv], [pltpu.VMEM((count, rows), F32)])


def grads_kernel(chunk, dh_ref, do_ref, w_ref, q_ref, o_ref, p_ref, stat_ref, far_ref, kv_ref, dq_ref, dqo_ref, dkv_ref):
    width = w_ref.shape[1]
    tokens = dh_ref.shape[0]
    d_hidden = jnp.concatenate([dh_ref[:, :width], do_ref[:, :width]], axis=0)
    d_out_w = nt(w_ref[...], d_hidden).astype(BF)
    parts = [d_out_w[h * HEAD_DIM : (h + 1) * HEAD_DIM, c * tokens : (c + 1) * tokens] for c in range(2) for h in range(2)]
    d_out_t = jnp.concatenate(parts, axis=1)
    d_out = jnp.concatenate([p.T for p in parts], axis=0)
    query = jnp.concatenate([heads_to_rows(q_ref[...]), heads_to_rows(o_ref[...])], axis=0)
    half = query.shape[0] // 2
    here = stat_ref[...]
    there = jnp.concatenate([far_ref[:, half:], far_ref[:, :half]], axis=1)
    top_here, top_there = here[HEAD_DIM : HEAD_DIM + 1], there[HEAD_DIM : HEAD_DIM + 1]
    top = jnp.maximum(top_here, top_there)
    in_here, in_there = jnp.exp(top_here - top), jnp.exp(top_there - top)
    total = here[HEAD_DIM + 1 : HEAD_DIM + 2] * in_here + there[HEAD_DIM + 1 : HEAD_DIM + 2] * in_there
    in_here, in_there = in_here / total, in_there / total
    out = here[:HEAD_DIM] * in_here + there[:HEAD_DIM] * in_there
    delta = jnp.sum(d_out_t.astype(F32) * out, axis=0, keepdims=True)
    d_query = jnp.zeros((HEAD_DIM, 2 * half), F32)
    for n in range(0, kv_ref.shape[0], chunk):
        span = slice(n, n + chunk)
        p = p_ref[span].astype(F32) * in_here
        d_probs = nn(kv_ref[span, HEAD_DIM:], d_out_t)
        ds = (p * (d_probs - delta)).astype(BF)
        dkv_ref[span, :HEAD_DIM] = (nn(ds, query) * SCALE).astype(BF)
        dkv_ref[span, HEAD_DIM:] = nn(p.astype(BF), d_out).astype(BF)
        d_query = d_query + tn(kv_ref[span, :HEAD_DIM], ds)
    d_query = (d_query * SCALE).T
    for ref, at in ((dq_ref, 0), (dqo_ref, half)):
        ref[:, :HEAD_DIM] = d_query[at : at + tokens]
        ref[:, HEAD_DIM:] = d_query[at + tokens : at + 2 * tokens]


def body(hidden, upstream, norm_gain, route_ids, route_weights, w_gate, w_up, w_down, w_out, queries, keys, values):
    ctx_count = lax.axis_size("context")
    exp_count = lax.axis_size("expert")
    tokens, width = hidden.shape
    chips = ctx_count // 2
    per = w_gate.shape[0]
    slots = ctx_count * PAIR
    z = lax.axis_index("expert")
    quarter = z % per
    q_arr = quarter.astype(jnp.int32).reshape(1)
    z_arr = z.astype(jnp.int32).reshape(1)
    gain = norm_gain.reshape(1, width)
    swap_core = [(i, i ^ 1) for i in range(ctx_count)]
    same_core = [[2 * i + k for i in range(chips)] for k in range(2)]

    def far(core):
        return -2 if core == 0 else 2

    def moves(step):
        return [
            (i * ctx_count + c, (i + step(c % 2)) % exp_count * ctx_count + c)
            for c in range(ctx_count)
            for i in range(exp_count)
        ]

    def trade(w, step):
        return lax.ppermute(w, ("expert", "context"), moves(step))

    leave = [((z + n) % per).astype(jnp.int32) for n in (1, per - 1, 2)]
    packs = pack(jnp.stack(leave[:2]), w_gate, w_up, w_down) + pack(jnp.stack(leave[2:]), w_gate, w_up, w_down)
    near_a, near_b = trade(packs[0], lambda core: 1), trade(packs[1], lambda core: -1)
    distant, near_a, near_b = lax.optimization_barrier((packs[2], near_a, near_b))
    got_far = trade(distant, far)

    ids = route_ids.T
    kv_head = z // (exp_count // 2)
    own_kv = jnp.concatenate(
        [lax.dynamic_slice_in_dim(a, kv_head * HEAD_DIM, HEAD_DIM, 1) for a in (keys, values)], axis=1)
    kv = lax.all_gather(own_kv, "context", axis=0, tiled=True, axis_index_groups=same_core)

    send, s0, sw0, sw1 = route(q_arr, per, ctx_count, ids, route_weights.T, hidden, upstream, gain)
    xy = lax.all_to_all(send.reshape(ctx_count, PAIR, width), "context", 0, 0, tiled=True)
    xy = xy.reshape(slots, width)
    narrow = width // 2 + 128
    near = expert_near(q_arr, xy, w_gate, w_up, w_down, near_a, near_b)
    rows = expert_far(xy, got_far, near)
    rows, kv = lax.optimization_barrier((rows, kv))
    rows = lax.all_to_all(rows.reshape(ctx_count, PAIR, narrow), "context", 0, 0, tiled=True)
    wide = width + 128
    q = on_chip(
        lambda *refs: gather_kernel(per, ctx_count, *refs), "gather_rows",
        jax.ShapeDtypeStruct((tokens, wide), BF),
        [q_arr], [rows.reshape(slots, narrow), s0, sw0, sw1, ids, hidden, gain])

    share = tokens // exp_count
    parts = (exp_count, share, wide)
    arrived = lax.all_to_all(q.reshape(parts), "expert", 0, 0, tiled=True)
    queries, q = lax.optimization_barrier((queries, q))
    other = lax.ppermute(queries, "context", swap_core)
    soft, stats = probs(queries, other, kv)
    far_stats = lax.ppermute(stats, "context", swap_core)
    arrived, far_stats = lax.optimization_barrier((arrived, far_stats))
    done = finish(z_arr, arrived, upstream)
    done = lax.all_to_all(done, "expert", 0, 0, tiled=True).reshape(tokens, wide)
    d_hidden = done[:, :width]
    d_route = done[:, width : width + route_ids.shape[1]].astype(F32)

    done_other = lax.ppermute(done, "context", swap_core)
    d_queries, d_other, part = on_chip(
        lambda *refs: grads_kernel(512, *refs), "attention_grads",
        [
            jax.ShapeDtypeStruct(queries.shape, F32),
            jax.ShapeDtypeStruct(queries.shape, F32),
            jax.ShapeDtypeStruct(kv.shape, BF),
        ],
        [], [done, done_other, w_out, queries, other, soft, stats, far_stats, kv], mib=GRADS_MIB)
    d_queries = d_queries + lax.ppermute(d_other, "context", swap_core)
    part = lax.all_to_all(
        part.reshape(chips, tokens, 2 * HEAD_DIM), "context", 0, 0, tiled=True, axis_index_groups=same_core)
    block = (exp_count, tokens, 2 * HEAD_DIM)
    part = on_chip(spread_kernel, "sum_chips", jax.ShapeDtypeStruct(block, BF), [], [part], mib=32)
    part = lax.all_to_all(part, "expert", 0, 0, tiled=True)
    d_keys, d_values = on_chip(
        last_kernel, "sum_heads", [jax.ShapeDtypeStruct((tokens, 2 * HEAD_DIM), F32)] * 2, [], [part], mib=32)
    return (d_hidden, d_route, d_queries, d_keys, d_values)


def solution(mesh):
    placed = (
        P("context", None),
        P("context", None),
        P(),
        P("context", None),
        P("context", None),
        P("context", None, "expert"),
        P("context", None, "expert"),
        P("context", "expert", None),
        P("expert", None),
        P("context", "expert"),
        P("context", None),
        P("context", None),
    )
    return jax.shard_map(
        body,
        mesh=mesh,
        in_specs=placed,
        out_specs=(
            P("context", None),
            P("context", None),
            P("context", "expert"),
            P("context", None),
            P("context", None),
        ),
        check_vma=False,
    )
```

```python
import math

import jax
import jax.numpy as jnp
from jax import lax
from jax.experimental import pallas as pl
from jax.experimental.pallas import tpu as pltpu
from jax.sharding import PartitionSpec as P

HEAD_DIM = 128
CAP = 12
BF = jnp.bfloat16
F32 = jnp.float32
PAIR = 2 * CAP
EPS = 1e-06
SCALE = 1.0 / math.sqrt(HEAD_DIM)
NT = (((1,), (1,)), ((), ()))
TN = (((0,), (0,)), ((), ()))
MB = 1 << 20
NEAR_MIB = 60
PACK_ROWS = 1024
PICK_COST = 30000000000
GRADS_ROWS = 1024
NEAR_TYPE = BF
NEAR_ROWS = 384
FAR_ROWS = 384
GRADS_MIB = 62
FINISH_MIB = 32
FAR_MIB = 60


def nt(a, b):
    return lax.dot_general(a, b, NT, preferred_element_type=F32)


def tn(a, b):
    return lax.dot_general(a, b, TN, preferred_element_type=F32)


def nn(a, b):
    return jnp.dot(a, b, preferred_element_type=F32)


def params(mib=60):
    return pltpu.CompilerParams(vmem_limit_bytes=mib * MB)


def whole(shape):
    return pl.BlockSpec(shape, lambda *_: (0,) * len(shape))


def row_expert(quarter, per, count, shape):
    row = lax.broadcasted_iota(jnp.int32, shape, 0)
    return jnp.where(row < count, row * per + quarter, -1)


def slot_split(shape, axis, first):
    slot = (lax.broadcasted_iota(jnp.int32, shape, axis) + first).astype(F32)
    lane = jnp.floor((slot + 0.5) * (1.0 / PAIR))
    rank = slot - PAIR * lane
    half = jnp.where(rank > CAP - 0.5, 1.0, 0.0)
    return lane, half, rank - CAP * half


def route_kernel(rows, per, count, q_ref, ids_ref, rw_ref, hid_ref, up_ref, gain_ref,
                 send_ref, s0_ref, sw0_ref, sw1_ref, m_ref, r_ref, w_ref, n_ref):
    step = pl.program_id(0)
    tokens = ids_ref.shape[1]

    @pl.when(step == 0)
    def _():
        ids = ids_ref[...]
        weights = rw_ref[...].astype(F32)
        named = row_expert(q_ref[0], per, count, (128, tokens))
        member = jnp.zeros((128, tokens), F32)
        weight = jnp.zeros((128, tokens), F32)
        for k in range(ids.shape[0]):
            hit = ids[k : k + 1] == named
            member = member + jnp.where(hit, 1.0, 0.0)
            weight = weight + jnp.where(hit, weights[k : k + 1], 0.0)
        m_ref[...] = member.astype(BF)
        w_ref[...] = weight.astype(BF)
        row = lax.broadcasted_iota(jnp.int32, (tokens, tokens), 0)
        col = lax.broadcasted_iota(jnp.int32, (tokens, tokens), 1)
        before = jnp.where(row < col, 1.0, 0.0).astype(BF)
        r_ref[...] = nn(member.astype(BF), before).astype(BF)
        wide = hid_ref[...].astype(F32)
        inv = lax.rsqrt(jnp.mean(wide * wide, axis=1, keepdims=True) + EPS)
        n_ref[:tokens] = (wide * inv * gain_ref[...]).astype(BF)
        n_ref[tokens:] = up_ref[...]

    lane_of, half_of, rank_of = slot_split((rows, 128), 0, step * rows)
    lane = lax.broadcasted_iota(jnp.int32, (rows, 128), 1).astype(F32)
    spread = jnp.where(lane == lane_of, 1.0, 0.0).astype(BF)
    chosen = (nn(spread, m_ref[...]) > 0.5) & (nn(spread, r_ref[...]) == rank_of)
    weight = nn(spread, w_ref[...])
    first, second = chosen & (half_of < 0.5), chosen & (half_of > 0.5)
    s0 = jnp.where(first, 1.0, 0.0).astype(BF)
    s1 = jnp.where(second, 1.0, 0.0).astype(BF)
    send_ref[...] = nn(jnp.concatenate([s0, s1], axis=1), n_ref[...]).astype(BF)
    s0_ref[...] = s0
    sw0_ref[...] = jnp.where(first, weight, 0.0).astype(BF)
    sw1_ref[...] = jnp.where(second, weight, 0.0).astype(BF)


def route(quarter, per, count, ids, weights, hidden, upstream, gain):
    tokens, width = hidden.shape
    rows = 256
    slots = count * PAIR
    matrix = pl.BlockSpec((rows, tokens), lambda i, p: (i, 0))
    return pl.pallas_call(
        lambda *refs: route_kernel(rows, per, count, *refs),
        grid_spec=pltpu.PrefetchScalarGridSpec(
            num_scalar_prefetch=1,
            grid=(slots // rows,),
            in_specs=[
                whole(ids.shape),
                whole(ids.shape),
                whole((tokens, width)),
                whole((tokens, width)),
                whole((1, width)),
            ],
            out_specs=[pl.BlockSpec((rows, width), lambda i, p: (i, 0)), matrix, matrix, matrix],
            scratch_shapes=[
                pltpu.VMEM((128, tokens), BF),
                pltpu.VMEM((128, tokens), BF),
                pltpu.VMEM((128, tokens), BF),
                pltpu.VMEM((2 * tokens, width), BF),
            ],
        ),
        out_shape=[jax.ShapeDtypeStruct((slots, width), BF)]
        + [jax.ShapeDtypeStruct((slots, tokens), BF)] * 3,
        compiler_params=params(),
        name="route",
    )(quarter, ids, weights, hidden, upstream, gain)


def pack_kernel(count, q_ref, *refs):
    for n in range(count):
        g_ref, u_ref, d_ref = refs[3 * n : 3 * n + 3]
        out_ref = refs[3 * count + n]
        unit = g_ref.shape[2]
        out_ref[0] = g_ref[0]
        out_ref[1] = u_ref[0]
        for k in range(d_ref.shape[2] // unit):
            out_ref[2, k * unit : (k + 1) * unit] = d_ref[0, :, k * unit : (k + 1) * unit]


def pack(which, w_gate, w_up, w_down):
    width, unit = w_gate.shape[1:]
    count = which.shape[0]
    rows = PACK_ROWS

    def at(n):
        tall = pl.BlockSpec((1, rows, unit), lambda i, q: (q[n], i, 0))
        return [tall, tall, pl.BlockSpec((1, unit, rows), lambda i, q: (q[n], 0, i))]

    return pl.pallas_call(
        lambda *refs: pack_kernel(count, *refs),
        grid_spec=pltpu.PrefetchScalarGridSpec(
            num_scalar_prefetch=1,
            grid=(width // rows,),
            in_specs=sum([at(n) for n in range(count)], []),
            out_specs=[pl.BlockSpec((3, rows, unit), lambda i, q: (0, i, 0))] * count,
        ),
        out_shape=[jax.ShapeDtypeStruct((3, width, unit), BF)] * count,
        compiler_params=params(),
        name="pack",
    )(which, *[w_gate, w_up, w_down] * count)


def pick_kernel(q_ref, w_ref, out_ref):
    out_ref[...] = w_ref[...]


def pick(which, w):
    _, unit, width = w.shape
    return pl.pallas_call(
        pick_kernel,
        grid_spec=pltpu.PrefetchScalarGridSpec(
            num_scalar_prefetch=1,
            grid=(1,),
            in_specs=[pl.BlockSpec((1, unit, width), lambda i, q: (q[0], 0, 0))],
            out_specs=whole((1, unit, width)),
        ),
        out_shape=jax.ShapeDtypeStruct((1, unit, width), BF),
        cost_estimate=pl.CostEstimate(flops=PICK_COST, bytes_accessed=2 * unit * width * 2, transcendentals=0),
        compiler_params=params(),
        name="pick",
    )(which, w)


def unpack(ref):
    unit = ref.shape[2]
    down = [ref[2, n * unit : (n + 1) * unit] for n in range(ref.shape[1] // unit)]
    return ref[0], ref[1], jnp.concatenate(down, axis=1)


def expert_rows(xy, w_in, w_down):
    rows, width = xy.shape
    half_width = width // 2
    ahead = nn(xy, w_in)
    gate, up = ahead[:, : w_in.shape[1] // 2], ahead[:, w_in.shape[1] // 2 :]
    proj = pltpu.roll(nt(xy, w_down), rows - CAP, 0)
    sig = 1.0 / (1.0 + jnp.exp(-gate))
    silu = gate * sig
    act = (silu * up).astype(BF).astype(F32)
    d_gate = (proj * up * (sig * (1.0 + gate * (1.0 - sig)))).astype(BF)
    d_up = (proj * silu).astype(BF)
    d_route = jnp.sum(act * proj, axis=1, keepdims=True)
    d_rows = nt(jnp.concatenate([d_gate, d_up], axis=1), w_in)
    _, half, _ = slot_split((rows, 1), 0, 0)
    out = jnp.where(half > 0.5, pltpu.roll(d_rows[:, half_width:], CAP, 0), d_rows[:, :half_width])
    return out, jnp.broadcast_to(d_route, (rows, 128))


def near_kernel(rows, q_ref, xy_ref, go_ref, uo_ref, do_ref, a_ref, b_ref, out_ref):
    width = xy_ref.shape[1]
    one, two = unpack(a_ref), unpack(b_ref)
    w_in = jnp.concatenate([go_ref[0], one[0], two[0], uo_ref[0], one[1], two[1]], axis=1)
    w_down = jnp.concatenate([do_ref[0], one[2], two[2]], axis=0)
    out, d_route = expert_rows(xy_ref[...], w_in, w_down)
    out_ref[:, : width // 2] = out.astype(NEAR_TYPE)
    out_ref[:, width // 2 :] = d_route.astype(NEAR_TYPE)


def expert_near(quarter, xy, w_gate, w_up, w_down, got_a, got_b):
    slots, width = xy.shape
    unit = w_gate.shape[2]
    rows = NEAR_ROWS
    own = pl.BlockSpec((1, width, unit), lambda i, p: (p[0], 0, 0))
    narrow = width // 2 + 128
    return pl.pallas_call(
        lambda *refs: near_kernel(rows, *refs),
        grid_spec=pltpu.PrefetchScalarGridSpec(
            num_scalar_prefetch=1,
            grid=(slots // rows,),
            in_specs=[
                pl.BlockSpec((rows, width), lambda i, p: (i, 0)),
                own,
                own,
                pl.BlockSpec((1, unit, width), lambda i, p: (p[0], 0, 0)),
                whole(got_a.shape),
                whole(got_b.shape),
            ],
            out_specs=pl.BlockSpec((rows, narrow), lambda i, p: (i, 0)),
        ),
        out_shape=jax.ShapeDtypeStruct((slots, narrow), NEAR_TYPE),
        compiler_params=params(NEAR_MIB),
        name="expert_near",
    )(quarter, xy, w_gate, w_up, w_down, got_a, got_b)


def far_kernel(xy_ref, in_ref, down_ref, near_ref, out_ref):
    width = xy_ref.shape[1]
    out, d_route = expert_rows(xy_ref[...], jnp.concatenate([in_ref[0], in_ref[1]], axis=1), down_ref[0])
    out_ref[:, : width // 2] = (near_ref[:, : width // 2] + out).astype(BF)
    out_ref[:, width // 2 :] = (near_ref[:, width // 2 :] + d_route).astype(BF)


def expert_far(xy, w_in, w_down, near):
    slots, width = xy.shape
    narrow = near.shape[1]
    rows = FAR_ROWS
    block = pl.BlockSpec((rows, narrow), lambda i: (i, 0))
    return pl.pallas_call(
        far_kernel,
        grid=(slots // rows,),
        in_specs=[pl.BlockSpec((rows, width), lambda i: (i, 0)), whole(w_in.shape), whole(w_down.shape), block],
        out_specs=block,
        out_shape=jax.ShapeDtypeStruct((slots, narrow), BF),
        compiler_params=params(FAR_MIB),
        name="expert_far",
    )(xy, w_in, w_down, near)


def gather_kernel(per, count, q_ref, back_ref, s0_ref, sw0_ref, sw1_ref, ids_ref, hid_ref, gain_ref, out_ref):
    tokens, width = hid_ref.shape
    half_width = width // 2
    wide = hid_ref[...].astype(F32)
    inv = lax.rsqrt(jnp.mean(wide * wide, axis=1, keepdims=True) + EPS)
    rows = back_ref[:, :half_width]
    d_normed = jnp.concatenate([tn(sw0_ref[...], rows), tn(sw1_ref[...], rows)], axis=1)
    g = d_normed * gain_ref[...]
    inner = jnp.mean(g * wide, axis=1, keepdims=True)
    out_ref[:, :width] = (inv * g - wide * (inv * inv * inv * inner)).astype(BF)
    slots = back_ref.shape[0]
    lane_of, _, _ = slot_split((slots, 128), 0, 0)
    lane = lax.broadcasted_iota(jnp.int32, (slots, 128), 1).astype(F32)
    placed = jnp.where(lane == lane_of, back_ref[:, half_width:].astype(F32), 0.0).astype(BF)
    route = tn(placed, s0_ref[...])
    named = row_expert(q_ref[0], per, count, (128, tokens))
    ids = ids_ref[...]
    row = lax.broadcasted_iota(jnp.int32, (128, tokens), 0)
    out = jnp.zeros((128, tokens), F32)
    for k in range(ids.shape[0]):
        value = jnp.sum(jnp.where(ids[k : k + 1] == named, route, 0.0), axis=0, keepdims=True)
        out = jnp.where(row == k, value, out)
    out_ref[:, width:] = out.T.astype(BF)


def on_chip(kernel, name, out_shape, scalars, arrays, scratch=(), mib=60):
    vmem = pl.BlockSpec(memory_space=pltpu.VMEM)
    many = isinstance(out_shape, list)
    return pl.pallas_call(
        kernel,
        in_specs=[pl.BlockSpec(memory_space=pltpu.SMEM)] * len(scalars) + [vmem] * len(arrays),
        out_specs=[vmem] * len(out_shape) if many else vmem,
        out_shape=out_shape,
        scratch_shapes=list(scratch),
        compiler_params=params(mib),
        name=name,
    )(*scalars, *arrays)


def sum_first(ref):
    total = ref[0].astype(F32)
    for n in range(1, ref.shape[0]):
        total = total + ref[n].astype(F32)
    return total


def finish_kernel(z_ref, in_ref, up_ref, out_ref):
    width = up_ref.shape[1]
    total = sum_first(in_ref)
    mine = up_ref[...].astype(F32)
    done = jnp.concatenate([total[:, :width] + mine, total[:, width:]], axis=1).astype(BF)
    for n in range(in_ref.shape[0]):
        out_ref[n] = done


def finish(z, arrived, upstream):
    parts, share, wide = arrived.shape
    return pl.pallas_call(
        finish_kernel,
        grid_spec=pltpu.PrefetchScalarGridSpec(
            num_scalar_prefetch=1,
            grid=(1,),
            in_specs=[
                whole((parts, share, wide)),
                pl.BlockSpec((share, upstream.shape[1]), lambda i, z: (z[0], 0)),
            ],
            out_specs=whole((parts, share, wide)),
        ),
        out_shape=jax.ShapeDtypeStruct((parts, share, wide), BF),
        compiler_params=params(FINISH_MIB),
        name="finish_hidden",
    )(z, arrived, upstream)


def spread_kernel(in_ref, out_ref):
    total = sum_first(in_ref).astype(BF)
    for n in range(out_ref.shape[0]):
        out_ref[n] = total


def last_kernel(in_ref, dk_ref, dv_ref):
    half = in_ref.shape[0] // 2
    for head in range(2):
        total = in_ref[head * half].astype(F32)
        for n in range(1, half):
            total = total + in_ref[head * half + n].astype(F32)
        at = slice(head * HEAD_DIM, (head + 1) * HEAD_DIM)
        dk_ref[:, at] = total[:, :HEAD_DIM]
        dv_ref[:, at] = total[:, HEAD_DIM:]


def heads_to_rows(x):
    return jnp.concatenate([x[:, :HEAD_DIM], x[:, HEAD_DIM:]], axis=0)


def probs_kernel(chunk, q_ref, o_ref, kv_ref, p_ref, stat_ref, s_ref):
    query = jnp.concatenate([heads_to_rows(q_ref[...]), heads_to_rows(o_ref[...])], axis=0)
    count = query.shape[0]
    steps = [slice(n, n + chunk) for n in range(0, kv_ref.shape[0], chunk)]
    top = None
    for span in steps:
        s = nt(kv_ref[span, :HEAD_DIM], query) * SCALE
        s_ref[span] = s
        most = jnp.max(s, axis=0, keepdims=True)
        top = most if top is None else jnp.maximum(top, most)
    total = jnp.zeros_like(top)
    out = jnp.zeros((HEAD_DIM, count), F32)
    for span in steps:
        e = jnp.exp(s_ref[span] - top)
        total = total + jnp.sum(e, axis=0, keepdims=True)
        p = e.astype(BF)
        p_ref[span] = p
        out = out + tn(kv_ref[span, HEAD_DIM:], p)
    stat_ref[:HEAD_DIM] = out
    row = lax.broadcasted_iota(jnp.int32, (8, count), 0)
    stat_ref[HEAD_DIM:] = jnp.where(row == 0, top, total)


def probs(queries, other, kv):
    count = kv.shape[0]
    rows = queries.shape[0] * 4
    return on_chip(
        lambda *refs: probs_kernel(512, *refs), "attention_probs",
        [jax.ShapeDtypeStruct((count, rows), BF), jax.ShapeDtypeStruct((HEAD_DIM + 8, rows), F32)],
        [], [queries, other, kv], [pltpu.VMEM((count, rows), F32)])


def grads_kernel(dh_ref, do_ref, w_ref, q_ref, o_ref, stat_ref, far_ref, p_ref, kv_ref,
                 dq_ref, dqo_ref, dkv_ref, t_ref, d_ref, row_ref, query_ref, sum_ref):
    step = pl.program_id(0)
    width = w_ref.shape[1]
    tokens = dh_ref.shape[0]
    half = sum_ref.shape[1] // 2

    @pl.when(step == 0)
    def _():
        d_hidden = jnp.concatenate([dh_ref[:, :width], do_ref[:, :width]], axis=0)
        d_out_w = nt(w_ref[...], d_hidden).astype(BF)
        parts = [d_out_w[h * HEAD_DIM : (h + 1) * HEAD_DIM, c * tokens : (c + 1) * tokens] for c in range(2) for h in range(2)]
        d_out_t = jnp.concatenate(parts, axis=1)
        t_ref[...] = d_out_t
        d_ref[...] = jnp.concatenate([p.T for p in parts], axis=0)
        query_ref[...] = jnp.concatenate([heads_to_rows(q_ref[...]), heads_to_rows(o_ref[...])], axis=0)
        here = stat_ref[...]
        there = jnp.concatenate([far_ref[:, half:], far_ref[:, :half]], axis=1)
        top_here, top_there = here[HEAD_DIM : HEAD_DIM + 1], there[HEAD_DIM : HEAD_DIM + 1]
        top = jnp.maximum(top_here, top_there)
        in_here, in_there = jnp.exp(top_here - top), jnp.exp(top_there - top)
        total = here[HEAD_DIM + 1 : HEAD_DIM + 2] * in_here + there[HEAD_DIM + 1 : HEAD_DIM + 2] * in_there
        in_here, in_there = in_here / total, in_there / total
        out = here[:HEAD_DIM] * in_here + there[:HEAD_DIM] * in_there
        row_ref[0:1] = in_here
        row_ref[1:2] = jnp.sum(d_out_t.astype(F32) * out, axis=0, keepdims=True)
        sum_ref[...] = jnp.zeros_like(sum_ref)

    p = p_ref[...].astype(F32) * row_ref[0:1]
    d_probs = nn(kv_ref[:, HEAD_DIM:], t_ref[...])
    ds = (p * (d_probs - row_ref[1:2])).astype(BF)
    dkv_ref[:, :HEAD_DIM] = (nn(ds, query_ref[...]) * SCALE).astype(BF)
    dkv_ref[:, HEAD_DIM:] = nn(p.astype(BF), d_ref[...]).astype(BF)
    sum_ref[...] += tn(kv_ref[:, :HEAD_DIM], ds)

    @pl.when(step == pl.num_programs(0) - 1)
    def _():
        d_query = (sum_ref[...] * SCALE).T
        for ref, at in ((dq_ref, 0), (dqo_ref, half)):
            ref[:, :HEAD_DIM] = d_query[at : at + tokens]
            ref[:, HEAD_DIM:] = d_query[at + tokens : at + 2 * tokens]


def grads(done, done_other, w_out, queries, other, stats, far_stats, soft, kv):
    chunk = GRADS_ROWS
    count, rows = soft.shape
    fixed = [done, done_other, w_out, queries, other, stats, far_stats]
    return pl.pallas_call(
        grads_kernel,
        grid=(count // chunk,),
        in_specs=[whole(a.shape) for a in fixed]
        + [pl.BlockSpec((chunk, rows), lambda i: (i, 0)), pl.BlockSpec((chunk, kv.shape[1]), lambda i: (i, 0))],
        out_specs=[whole(queries.shape)] * 2 + [pl.BlockSpec((chunk, kv.shape[1]), lambda i: (i, 0))],
        out_shape=[
            jax.ShapeDtypeStruct(queries.shape, F32),
            jax.ShapeDtypeStruct(queries.shape, F32),
            jax.ShapeDtypeStruct(kv.shape, BF),
        ],
        scratch_shapes=[
            pltpu.VMEM((HEAD_DIM, rows), BF),
            pltpu.VMEM((rows, HEAD_DIM), BF),
            pltpu.VMEM((8, rows), F32),
            pltpu.VMEM((rows, HEAD_DIM), BF),
            pltpu.VMEM((HEAD_DIM, rows), F32),
        ],
        compiler_params=params(GRADS_MIB),
        name="attention_grads",
    )(*fixed, soft, kv)


def body(hidden, upstream, norm_gain, route_ids, route_weights, w_gate, w_up, w_down, w_out, queries, keys, values):
    ctx_count = lax.axis_size("context")
    exp_count = lax.axis_size("expert")
    tokens, width = hidden.shape
    chips = ctx_count // 2
    per = w_gate.shape[0]
    slots = ctx_count * PAIR
    z = lax.axis_index("expert")
    quarter = z % per
    q_arr = quarter.astype(jnp.int32).reshape(1)
    z_arr = z.astype(jnp.int32).reshape(1)
    gain = norm_gain.reshape(1, width)
    swap_core = [(i, i ^ 1) for i in range(ctx_count)]
    same_core = [[2 * i + k for i in range(chips)] for k in range(2)]

    def far(core):
        return -2 if core == 0 else 2

    def moves(step):
        return [
            (i * ctx_count + c, (i + step(c % 2)) % exp_count * ctx_count + c)
            for c in range(ctx_count)
            for i in range(exp_count)
        ]

    def trade(w, step):
        return lax.ppermute(w, ("expert", "context"), moves(step))

    leave = jnp.stack([((z + n) % per).astype(jnp.int32) for n in (1, per - 1)])
    near_a, near_b = pack(leave, w_gate, w_up, w_down)
    near_a, near_b = trade(near_a, lambda core: 1), trade(near_b, lambda core: -1)
    which = ((z + 2) % per).astype(jnp.int32)
    far_in = trade(jnp.concatenate([lax.dynamic_slice_in_dim(w, which, 1, 0) for w in (w_gate, w_up)], axis=0), far)
    which, near_a, near_b = lax.optimization_barrier((which, near_a, near_b))
    far_down = trade(pick(which.reshape(1), w_down), far)

    ids = route_ids.T
    kv_head = z // (exp_count // 2)
    own_kv = jnp.concatenate(
        [lax.dynamic_slice_in_dim(a, kv_head * HEAD_DIM, HEAD_DIM, 1) for a in (keys, values)], axis=1)
    kv = lax.all_gather(own_kv, "context", axis=0, tiled=True, axis_index_groups=same_core)

    send, s0, sw0, sw1 = route(q_arr, per, ctx_count, ids, route_weights.T, hidden, upstream, gain)
    xy = lax.all_to_all(send.reshape(ctx_count, PAIR, width), "context", 0, 0, tiled=True)
    xy = xy.reshape(slots, width)
    narrow = width // 2 + 128
    near = expert_near(q_arr, xy, w_gate, w_up, w_down, near_a, near_b)
    rows = expert_far(xy, far_in, far_down, near)
    rows, kv = lax.optimization_barrier((rows, kv))
    rows = lax.all_to_all(rows.reshape(ctx_count, PAIR, narrow), "context", 0, 0, tiled=True)
    wide = width + 128
    q = on_chip(
        lambda *refs: gather_kernel(per, ctx_count, *refs), "gather_rows",
        jax.ShapeDtypeStruct((tokens, wide), BF),
        [q_arr], [rows.reshape(slots, narrow), s0, sw0, sw1, ids, hidden, gain])

    share = tokens // exp_count
    parts = (exp_count, share, wide)
    arrived = lax.all_to_all(q.reshape(parts), "expert", 0, 0, tiled=True)
    queries, q = lax.optimization_barrier((queries, q))
    other = lax.ppermute(queries, "context", swap_core)
    soft, stats = probs(queries, other, kv)
    far_stats = lax.ppermute(stats, "context", swap_core)
    arrived, far_stats = lax.optimization_barrier((arrived, far_stats))
    done = finish(z_arr, arrived, upstream)
    done = lax.all_to_all(done, "expert", 0, 0, tiled=True).reshape(tokens, wide)
    d_hidden = done[:, :width]
    d_route = done[:, width : width + route_ids.shape[1]].astype(F32)

    done_other = lax.ppermute(done, "context", swap_core)
    d_queries, d_other, part = grads(done, done_other, w_out, queries, other, stats, far_stats, soft, kv)
    d_queries = d_queries + lax.ppermute(d_other, "context", swap_core)
    part = lax.all_to_all(
        part.reshape(chips, tokens, 2 * HEAD_DIM), "context", 0, 0, tiled=True, axis_index_groups=same_core)
    block = (exp_count, tokens, 2 * HEAD_DIM)
    part = on_chip(spread_kernel, "sum_chips", jax.ShapeDtypeStruct(block, BF), [], [part], mib=32)
    part = lax.all_to_all(part, "expert", 0, 0, tiled=True)
    d_keys, d_values = on_chip(
        last_kernel, "sum_heads", [jax.ShapeDtypeStruct((tokens, 2 * HEAD_DIM), F32)] * 2, [], [part], mib=32)
    return (d_hidden, d_route, d_queries, d_keys, d_values)


def solution(mesh):
    placed = (
        P("context", None),
        P("context", None),
        P(),
        P("context", None),
        P("context", None),
        P("context", None, "expert"),
        P("context", None, "expert"),
        P("context", "expert", None),
        P("expert", None),
        P("context", "expert"),
        P("context", None),
        P("context", None),
    )
    return jax.shard_map(
        body,
        mesh=mesh,
        in_specs=placed,
        out_specs=(
            P("context", None),
            P("context", None),
            P("context", "expert"),
            P("context", None),
            P("context", None),
        ),
        check_vma=False,
    )
```

```python
import math

import jax
import jax.numpy as jnp
from jax import lax
from jax.experimental import pallas as pl
from jax.experimental.pallas import tpu as pltpu
from jax.sharding import PartitionSpec as P

HEAD_DIM = 128
CAP = 12
BF = jnp.bfloat16
F32 = jnp.float32
PAIR = 2 * CAP
EPS = 1e-06
SCALE = 1.0 / math.sqrt(HEAD_DIM)
NT = (((1,), (1,)), ((), ()))
TN = (((0,), (0,)), ((), ()))
MB = 1 << 20
NEAR_MIB = 60
PACK_ROWS = 1024
PICK_COST = 30000000000
NEAR_TYPE = BF
NEAR_ROWS = 384
FAR_ROWS = 384
GRADS_MIB = 36
FINISH_MIB = 32
FAR_MIB = 60


def nt(a, b):
    return lax.dot_general(a, b, NT, preferred_element_type=F32)


def tn(a, b):
    return lax.dot_general(a, b, TN, preferred_element_type=F32)


def nn(a, b):
    return jnp.dot(a, b, preferred_element_type=F32)


def params(mib=60):
    return pltpu.CompilerParams(vmem_limit_bytes=mib * MB)


def whole(shape):
    return pl.BlockSpec(shape, lambda *_: (0,) * len(shape))


def row_expert(quarter, per, count, shape):
    row = lax.broadcasted_iota(jnp.int32, shape, 0)
    return jnp.where(row < count, row * per + quarter, -1)


def slot_split(shape, axis, first):
    slot = (lax.broadcasted_iota(jnp.int32, shape, axis) + first).astype(F32)
    lane = jnp.floor((slot + 0.5) * (1.0 / PAIR))
    rank = slot - PAIR * lane
    half = jnp.where(rank > CAP - 0.5, 1.0, 0.0)
    return lane, half, rank - CAP * half


def route_kernel(rows, per, count, q_ref, ids_ref, rw_ref, hid_ref, up_ref, gain_ref,
                 send_ref, picks_ref, m_ref, r_ref, w_ref, n_ref):
    step = pl.program_id(0)
    tokens = ids_ref.shape[1]

    @pl.when(step == 0)
    def _():
        ids = ids_ref[...]
        weights = rw_ref[...].astype(F32)
        named = row_expert(q_ref[0], per, count, (128, tokens))
        member = jnp.zeros((128, tokens), F32)
        weight = jnp.zeros((128, tokens), F32)
        for k in range(ids.shape[0]):
            hit = ids[k : k + 1] == named
            member = member + jnp.where(hit, 1.0, 0.0)
            weight = weight + jnp.where(hit, weights[k : k + 1], 0.0)
        m_ref[...] = member.astype(BF)
        w_ref[...] = weight.astype(BF)
        row = lax.broadcasted_iota(jnp.int32, (tokens, tokens), 0)
        col = lax.broadcasted_iota(jnp.int32, (tokens, tokens), 1)
        before = jnp.where(row < col, 1.0, 0.0).astype(BF)
        r_ref[...] = nn(member.astype(BF), before).astype(BF)
        wide = hid_ref[...].astype(F32)
        inv = lax.rsqrt(jnp.mean(wide * wide, axis=1, keepdims=True) + EPS)
        n_ref[:tokens] = (wide * inv * gain_ref[...]).astype(BF)
        n_ref[tokens:] = up_ref[...]

    lane_of, half_of, rank_of = slot_split((rows, 128), 0, step * rows)
    lane = lax.broadcasted_iota(jnp.int32, (rows, 128), 1).astype(F32)
    spread = jnp.where(lane == lane_of, 1.0, 0.0).astype(BF)
    chosen = (nn(spread, m_ref[...]) > 0.5) & (nn(spread, r_ref[...]) == rank_of)
    weight = nn(spread, w_ref[...])
    first, second = chosen & (half_of < 0.5), chosen & (half_of > 0.5)
    s0 = jnp.where(first, 1.0, 0.0).astype(BF)
    s1 = jnp.where(second, 1.0, 0.0).astype(BF)
    send_ref[...] = nn(jnp.concatenate([s0, s1], axis=1), n_ref[...]).astype(BF)
    picks_ref[:, :128] = jnp.where(first, weight, 0.0).astype(BF)
    picks_ref[:, 128:256] = jnp.where(second, weight, 0.0).astype(BF)
    picks_ref[:, 256:] = s0


def route(quarter, per, count, ids, weights, hidden, upstream, gain):
    tokens, width = hidden.shape
    rows = 256
    slots = count * PAIR
    return pl.pallas_call(
        lambda *refs: route_kernel(rows, per, count, *refs),
        grid_spec=pltpu.PrefetchScalarGridSpec(
            num_scalar_prefetch=1,
            grid=(slots // rows,),
            in_specs=[
                whole(ids.shape),
                whole(ids.shape),
                whole((tokens, width)),
                whole((tokens, width)),
                whole((1, width)),
            ],
            out_specs=[
                pl.BlockSpec((rows, width), lambda i, p: (i, 0)),
                pl.BlockSpec((rows, 3 * tokens), lambda i, p: (i, 0)),
            ],
            scratch_shapes=[
                pltpu.VMEM((128, tokens), BF),
                pltpu.VMEM((128, tokens), BF),
                pltpu.VMEM((128, tokens), BF),
                pltpu.VMEM((2 * tokens, width), BF),
            ],
        ),
        out_shape=[jax.ShapeDtypeStruct((slots, width), BF), jax.ShapeDtypeStruct((slots, 3 * tokens), BF)],
        compiler_params=params(),
        name="route",
    )(quarter, ids, weights, hidden, upstream, gain)


def pack_kernel(count, q_ref, *refs):
    for n in range(count):
        g_ref, u_ref, d_ref = refs[3 * n : 3 * n + 3]
        out_ref = refs[3 * count + n]
        unit = g_ref.shape[2]
        out_ref[0] = g_ref[0]
        out_ref[1] = u_ref[0]
        for k in range(d_ref.shape[2] // unit):
            out_ref[2, k * unit : (k + 1) * unit] = d_ref[0, :, k * unit : (k + 1) * unit]


def pack(which, w_gate, w_up, w_down):
    width, unit = w_gate.shape[1:]
    count = which.shape[0]
    rows = PACK_ROWS

    def at(n):
        tall = pl.BlockSpec((1, rows, unit), lambda i, q: (q[n], i, 0))
        return [tall, tall, pl.BlockSpec((1, unit, rows), lambda i, q: (q[n], 0, i))]

    return pl.pallas_call(
        lambda *refs: pack_kernel(count, *refs),
        grid_spec=pltpu.PrefetchScalarGridSpec(
            num_scalar_prefetch=1,
            grid=(width // rows,),
            in_specs=sum([at(n) for n in range(count)], []),
            out_specs=[pl.BlockSpec((3, rows, unit), lambda i, q: (0, i, 0))] * count,
        ),
        out_shape=[jax.ShapeDtypeStruct((3, width, unit), BF)] * count,
        compiler_params=params(),
        name="pack",
    )(which, *[w_gate, w_up, w_down] * count)


def pick_kernel(q_ref, w_ref, out_ref):
    out_ref[...] = w_ref[...]


def pick(which, w):
    _, unit, width = w.shape
    return pl.pallas_call(
        pick_kernel,
        grid_spec=pltpu.PrefetchScalarGridSpec(
            num_scalar_prefetch=1,
            grid=(1,),
            in_specs=[pl.BlockSpec((1, unit, width), lambda i, q: (q[0], 0, 0))],
            out_specs=whole((1, unit, width)),
        ),
        out_shape=jax.ShapeDtypeStruct((1, unit, width), BF),
        cost_estimate=pl.CostEstimate(flops=PICK_COST, bytes_accessed=2 * unit * width * 2, transcendentals=0),
        compiler_params=params(),
        name="pick",
    )(which, w)


def unpack(ref):
    unit = ref.shape[2]
    down = [ref[2, n * unit : (n + 1) * unit] for n in range(ref.shape[1] // unit)]
    return ref[0], ref[1], jnp.concatenate(down, axis=1)


def expert_rows(xy, w_in, w_down):
    rows, width = xy.shape
    half_width = width // 2
    ahead = nn(xy, w_in)
    gate, up = ahead[:, : w_in.shape[1] // 2], ahead[:, w_in.shape[1] // 2 :]
    proj = pltpu.roll(nt(xy, w_down), rows - CAP, 0)
    sig = 1.0 / (1.0 + jnp.exp(-gate))
    silu = gate * sig
    act = (silu * up).astype(BF).astype(F32)
    d_gate = (proj * up * (sig * (1.0 + gate * (1.0 - sig)))).astype(BF)
    d_up = (proj * silu).astype(BF)
    d_route = jnp.sum(act * proj, axis=1, keepdims=True)
    d_rows = nt(jnp.concatenate([d_gate, d_up], axis=1), w_in)
    _, half, _ = slot_split((rows, 1), 0, 0)
    out = jnp.where(half > 0.5, pltpu.roll(d_rows[:, half_width:], CAP, 0), d_rows[:, :half_width])
    return out, jnp.broadcast_to(d_route, (rows, 128))


def near_kernel(rows, q_ref, xy_ref, go_ref, uo_ref, do_ref, a_ref, b_ref, out_ref):
    width = xy_ref.shape[1]
    one, two = unpack(a_ref), unpack(b_ref)
    w_in = jnp.concatenate([go_ref[0], one[0], two[0], uo_ref[0], one[1], two[1]], axis=1)
    w_down = jnp.concatenate([do_ref[0], one[2], two[2]], axis=0)
    out, d_route = expert_rows(xy_ref[...], w_in, w_down)
    out_ref[:, : width // 2] = out.astype(NEAR_TYPE)
    out_ref[:, width // 2 :] = d_route.astype(NEAR_TYPE)


def expert_near(quarter, xy, w_gate, w_up, w_down, got_a, got_b):
    slots, width = xy.shape
    unit = w_gate.shape[2]
    rows = NEAR_ROWS
    own = pl.BlockSpec((1, width, unit), lambda i, p: (p[0], 0, 0))
    narrow = width // 2 + 128
    return pl.pallas_call(
        lambda *refs: near_kernel(rows, *refs),
        grid_spec=pltpu.PrefetchScalarGridSpec(
            num_scalar_prefetch=1,
            grid=(slots // rows,),
            in_specs=[
                pl.BlockSpec((rows, width), lambda i, p: (i, 0)),
                own,
                own,
                pl.BlockSpec((1, unit, width), lambda i, p: (p[0], 0, 0)),
                whole(got_a.shape),
                whole(got_b.shape),
            ],
            out_specs=pl.BlockSpec((rows, narrow), lambda i, p: (i, 0)),
        ),
        out_shape=jax.ShapeDtypeStruct((slots, narrow), NEAR_TYPE),
        compiler_params=params(NEAR_MIB),
        name="expert_near",
    )(quarter, xy, w_gate, w_up, w_down, got_a, got_b)


def far_kernel(xy_ref, in_ref, down_ref, near_ref, out_ref):
    width = xy_ref.shape[1]
    out, d_route = expert_rows(xy_ref[...], jnp.concatenate([in_ref[0], in_ref[1]], axis=1), down_ref[0])
    out_ref[:, : width // 2] = (near_ref[:, : width // 2] + out).astype(BF)
    out_ref[:, width // 2 :] = (near_ref[:, width // 2 :] + d_route).astype(BF)


def expert_far(xy, w_in, w_down, near):
    slots, width = xy.shape
    narrow = near.shape[1]
    rows = FAR_ROWS
    block = pl.BlockSpec((rows, narrow), lambda i: (i, 0))
    return pl.pallas_call(
        far_kernel,
        grid=(slots // rows,),
        in_specs=[pl.BlockSpec((rows, width), lambda i: (i, 0)), whole(w_in.shape), whole(w_down.shape), block],
        out_specs=block,
        out_shape=jax.ShapeDtypeStruct((slots, narrow), BF),
        compiler_params=params(FAR_MIB),
        name="expert_far",
    )(xy, w_in, w_down, near)


def gather_kernel(per, count, q_ref, back_ref, picks_ref, ids_ref, hid_ref, gain_ref, out_ref):
    tokens, width = hid_ref.shape
    half_width = width // 2
    wide = hid_ref[...].astype(F32)
    inv = lax.rsqrt(jnp.mean(wide * wide, axis=1, keepdims=True) + EPS)
    rows = back_ref[:, :half_width]
    halves = tn(picks_ref[:, : 2 * tokens], rows)
    d_normed = jnp.concatenate([halves[:tokens], halves[tokens:]], axis=1)
    g = d_normed * gain_ref[...]
    inner = jnp.mean(g * wide, axis=1, keepdims=True)
    out_ref[:, :width] = (inv * g - wide * (inv * inv * inv * inner)).astype(BF)
    slots = back_ref.shape[0]
    lane_of, _, _ = slot_split((slots, 128), 0, 0)
    lane = lax.broadcasted_iota(jnp.int32, (slots, 128), 1).astype(F32)
    placed = jnp.where(lane == lane_of, back_ref[:, half_width:].astype(F32), 0.0).astype(BF)
    route = tn(placed, picks_ref[:, 2 * tokens :])
    named = row_expert(q_ref[0], per, count, (128, tokens))
    ids = ids_ref[...]
    row = lax.broadcasted_iota(jnp.int32, (128, tokens), 0)
    out = jnp.zeros((128, tokens), F32)
    for k in range(ids.shape[0]):
        value = jnp.sum(jnp.where(ids[k : k + 1] == named, route, 0.0), axis=0, keepdims=True)
        out = jnp.where(row == k, value, out)
    out_ref[:, width:] = out.T.astype(BF)


def on_chip(kernel, name, out_shape, scalars, arrays, scratch=(), mib=60):
    vmem = pl.BlockSpec(memory_space=pltpu.VMEM)
    many = isinstance(out_shape, list)
    return pl.pallas_call(
        kernel,
        in_specs=[pl.BlockSpec(memory_space=pltpu.SMEM)] * len(scalars) + [vmem] * len(arrays),
        out_specs=[vmem] * len(out_shape) if many else vmem,
        out_shape=out_shape,
        scratch_shapes=list(scratch),
        compiler_params=params(mib),
        name=name,
    )(*scalars, *arrays)


def sum_first(ref):
    total = ref[0].astype(F32)
    for n in range(1, ref.shape[0]):
        total = total + ref[n].astype(F32)
    return total


def finish_kernel(z_ref, in_ref, up_ref, out_ref):
    width = up_ref.shape[1]
    total = sum_first(in_ref)
    mine = up_ref[...].astype(F32)
    done = jnp.concatenate([total[:, :width] + mine, total[:, width:]], axis=1).astype(BF)
    for n in range(in_ref.shape[0]):
        out_ref[n] = done


def finish(z, arrived, upstream):
    parts, share, wide = arrived.shape
    return pl.pallas_call(
        finish_kernel,
        grid_spec=pltpu.PrefetchScalarGridSpec(
            num_scalar_prefetch=1,
            grid=(1,),
            in_specs=[
                whole((parts, share, wide)),
                pl.BlockSpec((share, upstream.shape[1]), lambda i, z: (z[0], 0)),
            ],
            out_specs=whole((parts, share, wide)),
        ),
        out_shape=jax.ShapeDtypeStruct((parts, share, wide), BF),
        compiler_params=params(FINISH_MIB),
        name="finish_hidden",
    )(z, arrived, upstream)


def spread_kernel(in_ref, out_ref):
    total = sum_first(in_ref).astype(BF)
    for n in range(out_ref.shape[0]):
        out_ref[n] = total


def last_kernel(in_ref, dk_ref, dv_ref):
    half = in_ref.shape[0] // 2
    for head in range(2):
        total = in_ref[head * half].astype(F32)
        for n in range(1, half):
            total = total + in_ref[head * half + n].astype(F32)
        at = slice(head * HEAD_DIM, (head + 1) * HEAD_DIM)
        dk_ref[:, at] = total[:, :HEAD_DIM]
        dv_ref[:, at] = total[:, HEAD_DIM:]


def heads_to_rows(x):
    return jnp.concatenate([x[:, :HEAD_DIM], x[:, HEAD_DIM:]], axis=0)


def probs_kernel(chunk, q_ref, o_ref, kv_ref, p_ref, stat_ref, s_ref):
    query = jnp.concatenate([heads_to_rows(q_ref[...]), heads_to_rows(o_ref[...])], axis=0)
    count = query.shape[0]
    steps = [slice(n, n + chunk) for n in range(0, kv_ref.shape[0], chunk)]
    top = None
    for span in steps:
        s = nt(kv_ref[span, :HEAD_DIM], query) * SCALE
        s_ref[span] = s
        most = jnp.max(s, axis=0, keepdims=True)
        top = most if top is None else jnp.maximum(top, most)
    total = jnp.zeros_like(top)
    out = jnp.zeros((HEAD_DIM, count), F32)
    for span in steps:
        e = jnp.exp(s_ref[span] - top)
        total = total + jnp.sum(e, axis=0, keepdims=True)
        p = e.astype(BF)
        p_ref[span] = p
        out = out + tn(kv_ref[span, HEAD_DIM:], p)
    stat_ref[:HEAD_DIM] = out
    row = lax.broadcasted_iota(jnp.int32, (8, count), 0)
    stat_ref[HEAD_DIM:] = jnp.where(row == 0, top, total)


def probs(queries, other, kv):
    count = kv.shape[0]
    rows = queries.shape[0] * 4
    return on_chip(
        lambda *refs: probs_kernel(512, *refs), "attention_probs",
        [jax.ShapeDtypeStruct((count, rows), BF), jax.ShapeDtypeStruct((HEAD_DIM + 8, rows), F32)],
        [], [queries, other, kv], [pltpu.VMEM((count, rows), F32)], mib=60)


def grads_kernel(chunk, dh_ref, do_ref, w_ref, q_ref, o_ref, p_ref, stat_ref, far_ref, kv_ref, dq_ref, dqo_ref, dkv_ref):
    width = w_ref.shape[1]
    tokens = dh_ref.shape[0]
    d_hidden = jnp.concatenate([dh_ref[:, :width], do_ref[:, :width]], axis=0)
    d_out_w = nt(w_ref[...], d_hidden).astype(BF)
    parts = [d_out_w[h * HEAD_DIM : (h + 1) * HEAD_DIM, c * tokens : (c + 1) * tokens] for c in range(2) for h in range(2)]
    d_out_t = jnp.concatenate(parts, axis=1)
    d_out = jnp.concatenate([p.T for p in parts], axis=0)
    query = jnp.concatenate([heads_to_rows(q_ref[...]), heads_to_rows(o_ref[...])], axis=0)
    half = query.shape[0] // 2
    here = stat_ref[...]
    there = jnp.concatenate([far_ref[:, half:], far_ref[:, :half]], axis=1)
    top_here, top_there = here[HEAD_DIM : HEAD_DIM + 1], there[HEAD_DIM : HEAD_DIM + 1]
    top = jnp.maximum(top_here, top_there)
    in_here, in_there = jnp.exp(top_here - top), jnp.exp(top_there - top)
    total = here[HEAD_DIM + 1 : HEAD_DIM + 2] * in_here + there[HEAD_DIM + 1 : HEAD_DIM + 2] * in_there
    in_here, in_there = in_here / total, in_there / total
    out = here[:HEAD_DIM] * in_here + there[:HEAD_DIM] * in_there
    delta = jnp.sum(d_out_t.astype(F32) * out, axis=0, keepdims=True)
    d_query = jnp.zeros((HEAD_DIM, 2 * half), F32)
    for n in range(0, kv_ref.shape[0], chunk):
        span = slice(n, n + chunk)
        p = p_ref[span].astype(F32) * in_here
        d_probs = nn(kv_ref[span, HEAD_DIM:], d_out_t)
        ds = (p * (d_probs - delta)).astype(BF)
        dkv_ref[span, :HEAD_DIM] = (nn(ds, query) * SCALE).astype(BF)
        dkv_ref[span, HEAD_DIM:] = nn(p.astype(BF), d_out).astype(BF)
        d_query = d_query + tn(kv_ref[span, :HEAD_DIM], ds)
    d_query = (d_query * SCALE).T
    for ref, at in ((dq_ref, 0), (dqo_ref, half)):
        ref[:, :HEAD_DIM] = d_query[at : at + tokens]
        ref[:, HEAD_DIM:] = d_query[at + tokens : at + 2 * tokens]


def body(hidden, upstream, norm_gain, route_ids, route_weights, w_gate, w_up, w_down, w_out, queries, keys, values):
    ctx_count = lax.axis_size("context")
    exp_count = lax.axis_size("expert")
    tokens, width = hidden.shape
    chips = ctx_count // 2
    per = w_gate.shape[0]
    slots = ctx_count * PAIR
    z = lax.axis_index("expert")
    quarter = z % per
    q_arr = quarter.astype(jnp.int32).reshape(1)
    z_arr = z.astype(jnp.int32).reshape(1)
    gain = norm_gain.reshape(1, width)
    swap_core = [(i, i ^ 1) for i in range(ctx_count)]
    same_core = [[2 * i + k for i in range(chips)] for k in range(2)]

    def far(core):
        return -2 if core == 0 else 2

    def moves(step):
        return [
            (i * ctx_count + c, (i + step(c % 2)) % exp_count * ctx_count + c)
            for c in range(ctx_count)
            for i in range(exp_count)
        ]

    def trade(w, step):
        return lax.ppermute(w, ("expert", "context"), moves(step))

    leave = jnp.stack([((z + n) % per).astype(jnp.int32) for n in (1, per - 1)])
    near_a, near_b = pack(leave, w_gate, w_up, w_down)
    near_a, near_b = trade(near_a, lambda core: 1), trade(near_b, lambda core: -1)
    which = ((z + 2) % per).astype(jnp.int32)
    far_in = trade(jnp.concatenate([lax.dynamic_slice_in_dim(w, which, 1, 0) for w in (w_gate, w_up)], axis=0), far)
    which, near_a, near_b = lax.optimization_barrier((which, near_a, near_b))
    far_down = trade(pick(which.reshape(1), w_down), far)

    ids = route_ids.T
    kv_head = z // (exp_count // 2)
    own_kv = jnp.concatenate(
        [lax.dynamic_slice_in_dim(a, kv_head * HEAD_DIM, HEAD_DIM, 1) for a in (keys, values)], axis=1)
    kv = lax.all_gather(own_kv, "context", axis=0, tiled=True, axis_index_groups=same_core)

    send, picks = route(q_arr, per, ctx_count, ids, route_weights.T, hidden, upstream, gain)
    xy = lax.all_to_all(send.reshape(ctx_count, PAIR, width), "context", 0, 0, tiled=True)
    xy = xy.reshape(slots, width)
    narrow = width // 2 + 128
    near = expert_near(q_arr, xy, w_gate, w_up, w_down, near_a, near_b)
    rows = expert_far(xy, far_in, far_down, near)
    rows, kv = lax.optimization_barrier((rows, kv))
    rows = lax.all_to_all(rows.reshape(ctx_count, PAIR, narrow), "context", 0, 0, tiled=True)
    wide = width + 128
    q = on_chip(
        lambda *refs: gather_kernel(per, ctx_count, *refs), "gather_rows",
        jax.ShapeDtypeStruct((tokens, wide), BF),
        [q_arr], [rows.reshape(slots, narrow), picks, ids, hidden, gain], mib=36)

    share = tokens // exp_count
    parts = (exp_count, share, wide)
    arrived = lax.all_to_all(q.reshape(parts), "expert", 0, 0, tiled=True)
    queries, q = lax.optimization_barrier((queries, q))
    other = lax.ppermute(queries, "context", swap_core)
    soft, stats = probs(queries, other, kv)
    far_stats = lax.ppermute(stats, "context", swap_core)
    arrived, far_stats = lax.optimization_barrier((arrived, far_stats))
    done = finish(z_arr, arrived, upstream)
    done = lax.all_to_all(done, "expert", 0, 0, tiled=True).reshape(tokens, wide)
    d_hidden = done[:, :width]
    d_route = done[:, width : width + route_ids.shape[1]].astype(F32)

    done_other = lax.ppermute(done, "context", swap_core)
    d_queries, d_other, part = on_chip(
        lambda *refs: grads_kernel(512, *refs), "attention_grads",
        [
            jax.ShapeDtypeStruct(queries.shape, F32),
            jax.ShapeDtypeStruct(queries.shape, F32),
            jax.ShapeDtypeStruct(kv.shape, BF),
        ],
        [], [done, done_other, w_out, queries, other, soft, stats, far_stats, kv], mib=GRADS_MIB)
    d_queries = d_queries + lax.ppermute(d_other, "context", swap_core)
    part = lax.all_to_all(
        part.reshape(chips, tokens, 2 * HEAD_DIM), "context", 0, 0, tiled=True, axis_index_groups=same_core)
    block = (exp_count, tokens, 2 * HEAD_DIM)
    part = on_chip(spread_kernel, "sum_chips", jax.ShapeDtypeStruct(block, BF), [], [part], mib=32)
    part = lax.all_to_all(part, "expert", 0, 0, tiled=True)
    d_keys, d_values = on_chip(
        last_kernel, "sum_heads", [jax.ShapeDtypeStruct((tokens, 2 * HEAD_DIM), F32)] * 2, [], [part], mib=32)
    return (d_hidden, d_route, d_queries, d_keys, d_values)


def solution(mesh):
    placed = (
        P("context", None),
        P("context", None),
        P(),
        P("context", None),
        P("context", None),
        P("context", None, "expert"),
        P("context", None, "expert"),
        P("context", "expert", None),
        P("expert", None),
        P("context", "expert"),
        P("context", None),
        P("context", None),
    )
    return jax.shard_map(
        body,
        mesh=mesh,
        in_specs=placed,
        out_specs=(
            P("context", None),
            P("context", None),
            P("context", "expert"),
            P("context", None),
            P("context", None),
        ),
        check_vma=False,
    )
```

```python
import math

import jax
import jax.numpy as jnp
from jax import lax
from jax.experimental import pallas as pl
from jax.experimental.pallas import tpu as pltpu
from jax.sharding import PartitionSpec as P

HEAD_DIM = 128
CAP = 12
BF = jnp.bfloat16
F32 = jnp.float32
PAIR = 2 * CAP
EPS = 1e-06
SCALE = 1.0 / math.sqrt(HEAD_DIM)
NT = (((1,), (1,)), ((), ()))
TN = (((0,), (0,)), ((), ()))
MB = 1 << 20
NEAR_MIB = 60
PACK_ROWS = 1024
PICK_COST = 30000000000
NEAR_TYPE = BF
NEAR_ROWS = 384
FAR_ROWS = 384
GRADS_MIB = 36
FINISH_MIB = 32
FAR_MIB = 60


def nt(a, b):
    return lax.dot_general(a, b, NT, preferred_element_type=F32)


def tn(a, b):
    return lax.dot_general(a, b, TN, preferred_element_type=F32)


def nn(a, b):
    return jnp.dot(a, b, preferred_element_type=F32)


def params(mib=60):
    return pltpu.CompilerParams(vmem_limit_bytes=mib * MB)


def whole(shape):
    return pl.BlockSpec(shape, lambda *_: (0,) * len(shape))


def row_expert(quarter, per, count, shape):
    row = lax.broadcasted_iota(jnp.int32, shape, 0)
    return jnp.where(row < count, row * per + quarter, -1)


def slot_split(shape, axis, first):
    slot = (lax.broadcasted_iota(jnp.int32, shape, axis) + first).astype(F32)
    lane = jnp.floor((slot + 0.5) * (1.0 / PAIR))
    rank = slot - PAIR * lane
    half = jnp.where(rank > CAP - 0.5, 1.0, 0.0)
    return lane, half, rank - CAP * half


def route_kernel(rows, per, count, q_ref, ids_ref, rw_ref, hid_ref, up_ref, gain_ref,
                 send_ref, picks_ref, m_ref, r_ref, w_ref, n_ref):
    step = pl.program_id(0)
    tokens = ids_ref.shape[1]

    @pl.when(step == 0)
    def _():
        ids = ids_ref[...]
        weights = rw_ref[...].astype(F32)
        named = row_expert(q_ref[0], per, count, (128, tokens))
        member = jnp.zeros((128, tokens), F32)
        weight = jnp.zeros((128, tokens), F32)
        for k in range(ids.shape[0]):
            hit = ids[k : k + 1] == named
            member = member + jnp.where(hit, 1.0, 0.0)
            weight = weight + jnp.where(hit, weights[k : k + 1], 0.0)
        m_ref[...] = member.astype(BF)
        w_ref[...] = weight.astype(BF)
        row = lax.broadcasted_iota(jnp.int32, (tokens, tokens), 0)
        col = lax.broadcasted_iota(jnp.int32, (tokens, tokens), 1)
        before = jnp.where(row < col, 1.0, 0.0).astype(BF)
        r_ref[...] = nn(member.astype(BF), before).astype(BF)
        wide = hid_ref[...].astype(F32)
        inv = lax.rsqrt(jnp.mean(wide * wide, axis=1, keepdims=True) + EPS)
        n_ref[:tokens] = (wide * inv * gain_ref[...]).astype(BF)
        n_ref[tokens:] = up_ref[...]

    lane_of, half_of, rank_of = slot_split((rows, 128), 0, step * rows)
    lane = lax.broadcasted_iota(jnp.int32, (rows, 128), 1).astype(F32)
    spread = jnp.where(lane == lane_of, 1.0, 0.0).astype(BF)
    chosen = (nn(spread, m_ref[...]) > 0.5) & (nn(spread, r_ref[...]) == rank_of)
    weight = nn(spread, w_ref[...])
    first, second = chosen & (half_of < 0.5), chosen & (half_of > 0.5)
    s0 = jnp.where(first, 1.0, 0.0).astype(BF)
    s1 = jnp.where(second, 1.0, 0.0).astype(BF)
    send_ref[...] = nn(jnp.concatenate([s0, s1], axis=1), n_ref[...]).astype(BF)
    picks_ref[:, :128] = jnp.where(first, weight, 0.0).astype(BF)
    picks_ref[:, 128:256] = jnp.where(second, weight, 0.0).astype(BF)
    picks_ref[:, 256:] = s0


def route(quarter, per, count, ids, weights, hidden, upstream, gain):
    tokens, width = hidden.shape
    rows = 256
    slots = count * PAIR
    return pl.pallas_call(
        lambda *refs: route_kernel(rows, per, count, *refs),
        grid_spec=pltpu.PrefetchScalarGridSpec(
            num_scalar_prefetch=1,
            grid=(slots // rows,),
            in_specs=[
                whole(ids.shape),
                whole(ids.shape),
                whole((tokens, width)),
                whole((tokens, width)),
                whole((1, width)),
            ],
            out_specs=[
                pl.BlockSpec((rows, width), lambda i, p: (i, 0)),
                pl.BlockSpec((rows, 3 * tokens), lambda i, p: (i, 0)),
            ],
            scratch_shapes=[
                pltpu.VMEM((128, tokens), BF),
                pltpu.VMEM((128, tokens), BF),
                pltpu.VMEM((128, tokens), BF),
                pltpu.VMEM((2 * tokens, width), BF),
            ],
        ),
        out_shape=[jax.ShapeDtypeStruct((slots, width), BF), jax.ShapeDtypeStruct((slots, 3 * tokens), BF)],
        compiler_params=params(),
        name="route",
    )(quarter, ids, weights, hidden, upstream, gain)


def pack_kernel(count, q_ref, *refs):
    for n in range(count):
        g_ref, u_ref, d_ref = refs[3 * n : 3 * n + 3]
        out_ref = refs[3 * count + n]
        unit = g_ref.shape[2]
        out_ref[0] = g_ref[0]
        out_ref[1] = u_ref[0]
        for k in range(d_ref.shape[2] // unit):
            out_ref[2, k * unit : (k + 1) * unit] = d_ref[0, :, k * unit : (k + 1) * unit]


def pack(which, w_gate, w_up, w_down):
    width, unit = w_gate.shape[1:]
    count = which.shape[0]
    rows = PACK_ROWS

    def at(n):
        tall = pl.BlockSpec((1, rows, unit), lambda i, q: (q[n], i, 0))
        return [tall, tall, pl.BlockSpec((1, unit, rows), lambda i, q: (q[n], 0, i))]

    return pl.pallas_call(
        lambda *refs: pack_kernel(count, *refs),
        grid_spec=pltpu.PrefetchScalarGridSpec(
            num_scalar_prefetch=1,
            grid=(width // rows,),
            in_specs=sum([at(n) for n in range(count)], []),
            out_specs=[pl.BlockSpec((3, rows, unit), lambda i, q: (0, i, 0))] * count,
        ),
        out_shape=[jax.ShapeDtypeStruct((3, width, unit), BF)] * count,
        compiler_params=params(),
        name="pack",
    )(which, *[w_gate, w_up, w_down] * count)


def pick_kernel(q_ref, w_ref, out_ref):
    out_ref[...] = w_ref[...]


def pick(which, w):
    _, unit, width = w.shape
    return pl.pallas_call(
        pick_kernel,
        grid_spec=pltpu.PrefetchScalarGridSpec(
            num_scalar_prefetch=1,
            grid=(1,),
            in_specs=[pl.BlockSpec((1, unit, width), lambda i, q: (q[0], 0, 0))],
            out_specs=whole((1, unit, width)),
        ),
        out_shape=jax.ShapeDtypeStruct((1, unit, width), BF),
        cost_estimate=pl.CostEstimate(flops=PICK_COST, bytes_accessed=2 * unit * width * 2, transcendentals=0),
        compiler_params=params(),
        name="pick",
    )(which, w)


def unpack(ref):
    unit = ref.shape[2]
    down = [ref[2, n * unit : (n + 1) * unit] for n in range(ref.shape[1] // unit)]
    return ref[0], ref[1], jnp.concatenate(down, axis=1)


def expert_rows(xy, w_in, w_down):
    rows, width = xy.shape
    half_width = width // 2
    ahead = nn(xy, w_in)
    gate, up = ahead[:, : w_in.shape[1] // 2], ahead[:, w_in.shape[1] // 2 :]
    proj = pltpu.roll(nt(xy, w_down), rows - CAP, 0)
    sig = 1.0 / (1.0 + jnp.exp(-gate))
    silu = gate * sig
    act = (silu * up).astype(BF).astype(F32)
    d_gate = (proj * up * (sig * (1.0 + gate * (1.0 - sig)))).astype(BF)
    d_up = (proj * silu).astype(BF)
    d_route = jnp.sum(act * proj, axis=1, keepdims=True)
    d_rows = nt(jnp.concatenate([d_gate, d_up], axis=1), w_in)
    _, half, _ = slot_split((rows, 1), 0, 0)
    out = jnp.where(half > 0.5, pltpu.roll(d_rows[:, half_width:], CAP, 0), d_rows[:, :half_width])
    return out, jnp.broadcast_to(d_route, (rows, 128))


def near_kernel(rows, q_ref, xy_ref, go_ref, uo_ref, do_ref, a_ref, b_ref, out_ref):
    width = xy_ref.shape[1]
    one, two = unpack(a_ref), unpack(b_ref)
    w_in = jnp.concatenate([go_ref[0], one[0], two[0], uo_ref[0], one[1], two[1]], axis=1)
    w_down = jnp.concatenate([do_ref[0], one[2], two[2]], axis=0)
    out, d_route = expert_rows(xy_ref[...], w_in, w_down)
    out_ref[:, : width // 2] = out.astype(NEAR_TYPE)
    out_ref[:, width // 2 :] = d_route.astype(NEAR_TYPE)


def expert_near(quarter, xy, w_gate, w_up, own_down, got_a, got_b):
    slots, width = xy.shape
    unit = w_gate.shape[2]
    rows = NEAR_ROWS
    own = pl.BlockSpec((1, width, unit), lambda i, p: (p[0], 0, 0))
    narrow = width // 2 + 128
    return pl.pallas_call(
        lambda *refs: near_kernel(rows, *refs),
        grid_spec=pltpu.PrefetchScalarGridSpec(
            num_scalar_prefetch=1,
            grid=(slots // rows,),
            in_specs=[
                pl.BlockSpec((rows, width), lambda i, p: (i, 0)),
                own,
                own,
                whole((1, unit, width)),
                whole(got_a.shape),
                whole(got_b.shape),
            ],
            out_specs=pl.BlockSpec((rows, narrow), lambda i, p: (i, 0)),
        ),
        out_shape=jax.ShapeDtypeStruct((slots, narrow), NEAR_TYPE),
        compiler_params=params(NEAR_MIB),
        name="expert_near",
    )(quarter, xy, w_gate, w_up, own_down, got_a, got_b)


def far_kernel(xy_ref, in_ref, down_ref, near_ref, out_ref):
    width = xy_ref.shape[1]
    out, d_route = expert_rows(xy_ref[...], jnp.concatenate([in_ref[0], in_ref[1]], axis=1), down_ref[0])
    out_ref[:, : width // 2] = (near_ref[:, : width // 2] + out).astype(BF)
    out_ref[:, width // 2 :] = (near_ref[:, width // 2 :] + d_route).astype(BF)


def expert_far(xy, w_in, w_down, near):
    slots, width = xy.shape
    narrow = near.shape[1]
    rows = FAR_ROWS
    block = pl.BlockSpec((rows, narrow), lambda i: (i, 0))
    return pl.pallas_call(
        far_kernel,
        grid=(slots // rows,),
        in_specs=[pl.BlockSpec((rows, width), lambda i: (i, 0)), whole(w_in.shape), whole(w_down.shape), block],
        out_specs=block,
        out_shape=jax.ShapeDtypeStruct((slots, narrow), BF),
        compiler_params=params(FAR_MIB),
        name="expert_far",
    )(xy, w_in, w_down, near)


def gather_kernel(per, count, q_ref, back_ref, picks_ref, ids_ref, hid_ref, gain_ref, out_ref):
    tokens, width = hid_ref.shape
    half_width = width // 2
    wide = hid_ref[...].astype(F32)
    inv = lax.rsqrt(jnp.mean(wide * wide, axis=1, keepdims=True) + EPS)
    rows = back_ref[:, :half_width]
    halves = tn(picks_ref[:, : 2 * tokens], rows)
    d_normed = jnp.concatenate([halves[:tokens], halves[tokens:]], axis=1)
    g = d_normed * gain_ref[...]
    inner = jnp.mean(g * wide, axis=1, keepdims=True)
    out_ref[:, :width] = (inv * g - wide * (inv * inv * inv * inner)).astype(BF)
    slots = back_ref.shape[0]
    lane_of, _, _ = slot_split((slots, 128), 0, 0)
    lane = lax.broadcasted_iota(jnp.int32, (slots, 128), 1).astype(F32)
    placed = jnp.where(lane == lane_of, back_ref[:, half_width:].astype(F32), 0.0).astype(BF)
    route = tn(placed, picks_ref[:, 2 * tokens :])
    named = row_expert(q_ref[0], per, count, (128, tokens))
    ids = ids_ref[...]
    row = lax.broadcasted_iota(jnp.int32, (128, tokens), 0)
    out = jnp.zeros((128, tokens), F32)
    for k in range(ids.shape[0]):
        value = jnp.sum(jnp.where(ids[k : k + 1] == named, route, 0.0), axis=0, keepdims=True)
        out = jnp.where(row == k, value, out)
    out_ref[:, width:] = out.T.astype(BF)


def on_chip(kernel, name, out_shape, scalars, arrays, scratch=(), mib=60):
    vmem = pl.BlockSpec(memory_space=pltpu.VMEM)
    many = isinstance(out_shape, list)
    return pl.pallas_call(
        kernel,
        in_specs=[pl.BlockSpec(memory_space=pltpu.SMEM)] * len(scalars) + [vmem] * len(arrays),
        out_specs=[vmem] * len(out_shape) if many else vmem,
        out_shape=out_shape,
        scratch_shapes=list(scratch),
        compiler_params=params(mib),
        name=name,
    )(*scalars, *arrays)


def sum_first(ref):
    total = ref[0].astype(F32)
    for n in range(1, ref.shape[0]):
        total = total + ref[n].astype(F32)
    return total


def finish_kernel(z_ref, in_ref, up_ref, out_ref):
    width = up_ref.shape[1]
    total = sum_first(in_ref)
    mine = up_ref[...].astype(F32)
    done = jnp.concatenate([total[:, :width] + mine, total[:, width:]], axis=1).astype(BF)
    for n in range(in_ref.shape[0]):
        out_ref[n] = done


def finish(z, arrived, upstream):
    parts, share, wide = arrived.shape
    return pl.pallas_call(
        finish_kernel,
        grid_spec=pltpu.PrefetchScalarGridSpec(
            num_scalar_prefetch=1,
            grid=(1,),
            in_specs=[
                whole((parts, share, wide)),
                pl.BlockSpec((share, upstream.shape[1]), lambda i, z: (z[0], 0)),
            ],
            out_specs=whole((parts, share, wide)),
        ),
        out_shape=jax.ShapeDtypeStruct((parts, share, wide), BF),
        compiler_params=params(FINISH_MIB),
        name="finish_hidden",
    )(z, arrived, upstream)


def spread_kernel(in_ref, out_ref):
    total = sum_first(in_ref).astype(BF)
    for n in range(out_ref.shape[0]):
        out_ref[n] = total


def last_kernel(in_ref, dk_ref, dv_ref):
    half = in_ref.shape[0] // 2
    for head in range(2):
        total = in_ref[head * half].astype(F32)
        for n in range(1, half):
            total = total + in_ref[head * half + n].astype(F32)
        at = slice(head * HEAD_DIM, (head + 1) * HEAD_DIM)
        dk_ref[:, at] = total[:, :HEAD_DIM]
        dv_ref[:, at] = total[:, HEAD_DIM:]


def heads_to_rows(x):
    return jnp.concatenate([x[:, :HEAD_DIM], x[:, HEAD_DIM:]], axis=0)


def probs_kernel(chunk, q_ref, o_ref, kv_ref, p_ref, stat_ref, s_ref):
    query = jnp.concatenate([heads_to_rows(q_ref[...]), heads_to_rows(o_ref[...])], axis=0)
    count = query.shape[0]
    steps = [slice(n, n + chunk) for n in range(0, kv_ref.shape[0], chunk)]
    top = None
    for span in steps:
        s = nt(kv_ref[span, :HEAD_DIM], query) * SCALE
        s_ref[span] = s
        most = jnp.max(s, axis=0, keepdims=True)
        top = most if top is None else jnp.maximum(top, most)
    total = jnp.zeros_like(top)
    out = jnp.zeros((HEAD_DIM, count), F32)
    for span in steps:
        e = jnp.exp(s_ref[span] - top)
        total = total + jnp.sum(e, axis=0, keepdims=True)
        p = e.astype(BF)
        p_ref[span] = p
        out = out + tn(kv_ref[span, HEAD_DIM:], p)
    stat_ref[:HEAD_DIM] = out
    row = lax.broadcasted_iota(jnp.int32, (8, count), 0)
    stat_ref[HEAD_DIM:] = jnp.where(row == 0, top, total)


def probs(queries, other, kv):
    count = kv.shape[0]
    rows = queries.shape[0] * 4
    return on_chip(
        lambda *refs: probs_kernel(512, *refs), "attention_probs",
        [jax.ShapeDtypeStruct((count, rows), BF), jax.ShapeDtypeStruct((HEAD_DIM + 8, rows), F32)],
        [], [queries, other, kv], [pltpu.VMEM((count, rows), F32)], mib=60)


def grads_kernel(chunk, dh_ref, do_ref, w_ref, q_ref, o_ref, p_ref, stat_ref, far_ref, kv_ref, dq_ref, dqo_ref, dkv_ref):
    width = w_ref.shape[1]
    tokens = dh_ref.shape[0]
    d_hidden = jnp.concatenate([dh_ref[:, :width], do_ref[:, :width]], axis=0)
    d_out_w = nt(w_ref[...], d_hidden).astype(BF)
    parts = [d_out_w[h * HEAD_DIM : (h + 1) * HEAD_DIM, c * tokens : (c + 1) * tokens] for c in range(2) for h in range(2)]
    d_out_t = jnp.concatenate(parts, axis=1)
    d_out = jnp.concatenate([p.T for p in parts], axis=0)
    query = jnp.concatenate([heads_to_rows(q_ref[...]), heads_to_rows(o_ref[...])], axis=0)
    half = query.shape[0] // 2
    here = stat_ref[...]
    there = jnp.concatenate([far_ref[:, half:], far_ref[:, :half]], axis=1)
    top_here, top_there = here[HEAD_DIM : HEAD_DIM + 1], there[HEAD_DIM : HEAD_DIM + 1]
    top = jnp.maximum(top_here, top_there)
    in_here, in_there = jnp.exp(top_here - top), jnp.exp(top_there - top)
    total = here[HEAD_DIM + 1 : HEAD_DIM + 2] * in_here + there[HEAD_DIM + 1 : HEAD_DIM + 2] * in_there
    in_here, in_there = in_here / total, in_there / total
    out = here[:HEAD_DIM] * in_here + there[:HEAD_DIM] * in_there
    delta = jnp.sum(d_out_t.astype(F32) * out, axis=0, keepdims=True)
    d_query = jnp.zeros((HEAD_DIM, 2 * half), F32)
    for n in range(0, kv_ref.shape[0], chunk):
        span = slice(n, n + chunk)
        p = p_ref[span].astype(F32) * in_here
        d_probs = nn(kv_ref[span, HEAD_DIM:], d_out_t)
        ds = (p * (d_probs - delta)).astype(BF)
        dkv_ref[span, :HEAD_DIM] = (nn(ds, query) * SCALE).astype(BF)
        dkv_ref[span, HEAD_DIM:] = nn(p.astype(BF), d_out).astype(BF)
        d_query = d_query + tn(kv_ref[span, :HEAD_DIM], ds)
    d_query = (d_query * SCALE).T
    for ref, at in ((dq_ref, 0), (dqo_ref, half)):
        ref[:, :HEAD_DIM] = d_query[at : at + tokens]
        ref[:, HEAD_DIM:] = d_query[at + tokens : at + 2 * tokens]


def body(hidden, upstream, norm_gain, route_ids, route_weights, w_gate, w_up, w_down, w_out, queries, keys, values):
    ctx_count = lax.axis_size("context")
    exp_count = lax.axis_size("expert")
    tokens, width = hidden.shape
    chips = ctx_count // 2
    per = w_gate.shape[0]
    slots = ctx_count * PAIR
    z = lax.axis_index("expert")
    quarter = z % per
    q_arr = quarter.astype(jnp.int32).reshape(1)
    z_arr = z.astype(jnp.int32).reshape(1)
    gain = norm_gain.reshape(1, width)
    swap_core = [(i, i ^ 1) for i in range(ctx_count)]
    same_core = [[2 * i + k for i in range(chips)] for k in range(2)]

    def far(core):
        return -2 if core == 0 else 2

    def moves(step):
        return [
            (i * ctx_count + c, (i + step(c % 2)) % exp_count * ctx_count + c)
            for c in range(ctx_count)
            for i in range(exp_count)
        ]

    def trade(w, step):
        return lax.ppermute(w, ("expert", "context"), moves(step))

    leave = jnp.stack([((z + n) % per).astype(jnp.int32) for n in (1, per - 1)])
    near_a, near_b = pack(leave, w_gate, w_up, w_down)
    near_a, near_b = trade(near_a, lambda core: 1), trade(near_b, lambda core: -1)
    far_gate, far_up, far_down = [lax.dynamic_slice_in_dim(w, (z + 2) % per, 1, 0) for w in (w_gate, w_up, w_down)]
    far_in = trade(jnp.concatenate([far_gate, far_up], axis=0), far)
    far_down = trade(far_down, far)
    mine, near_a, near_b = lax.optimization_barrier((q_arr, near_a, near_b))
    own_down = pick(mine, w_down)

    ids = route_ids.T
    kv_head = z // (exp_count // 2)
    own_kv = jnp.concatenate(
        [lax.dynamic_slice_in_dim(a, kv_head * HEAD_DIM, HEAD_DIM, 1) for a in (keys, values)], axis=1)
    kv = lax.all_gather(own_kv, "context", axis=0, tiled=True, axis_index_groups=same_core)

    send, picks = route(q_arr, per, ctx_count, ids, route_weights.T, hidden, upstream, gain)
    xy = lax.all_to_all(send.reshape(ctx_count, PAIR, width), "context", 0, 0, tiled=True)
    xy = xy.reshape(slots, width)
    narrow = width // 2 + 128
    near = expert_near(q_arr, xy, w_gate, w_up, own_down, near_a, near_b)
    rows = expert_far(xy, far_in, far_down, near)
    rows, kv = lax.optimization_barrier((rows, kv))
    rows = lax.all_to_all(rows.reshape(ctx_count, PAIR, narrow), "context", 0, 0, tiled=True)
    wide = width + 128
    q = on_chip(
        lambda *refs: gather_kernel(per, ctx_count, *refs), "gather_rows",
        jax.ShapeDtypeStruct((tokens, wide), BF),
        [q_arr], [rows.reshape(slots, narrow), picks, ids, hidden, gain], mib=36)

    share = tokens // exp_count
    parts = (exp_count, share, wide)
    arrived = lax.all_to_all(q.reshape(parts), "expert", 0, 0, tiled=True)
    queries, q = lax.optimization_barrier((queries, q))
    other = lax.ppermute(queries, "context", swap_core)
    soft, stats = probs(queries, other, kv)
    far_stats = lax.ppermute(stats, "context", swap_core)
    arrived, far_stats = lax.optimization_barrier((arrived, far_stats))
    done = finish(z_arr, arrived, upstream)
    done = lax.all_to_all(done, "expert", 0, 0, tiled=True).reshape(tokens, wide)
    d_hidden = done[:, :width]
    d_route = done[:, width : width + route_ids.shape[1]].astype(F32)

    done_other = lax.ppermute(done, "context", swap_core)
    d_queries, d_other, part = on_chip(
        lambda *refs: grads_kernel(512, *refs), "attention_grads",
        [
            jax.ShapeDtypeStruct(queries.shape, F32),
            jax.ShapeDtypeStruct(queries.shape, F32),
            jax.ShapeDtypeStruct(kv.shape, BF),
        ],
        [], [done, done_other, w_out, queries, other, soft, stats, far_stats, kv], mib=GRADS_MIB)
    d_queries = d_queries + lax.ppermute(d_other, "context", swap_core)
    part = lax.all_to_all(
        part.reshape(chips, tokens, 2 * HEAD_DIM), "context", 0, 0, tiled=True, axis_index_groups=same_core)
    block = (exp_count, tokens, 2 * HEAD_DIM)
    part = on_chip(spread_kernel, "sum_chips", jax.ShapeDtypeStruct(block, BF), [], [part], mib=32)
    part = lax.all_to_all(part, "expert", 0, 0, tiled=True)
    d_keys, d_values = on_chip(
        last_kernel, "sum_heads", [jax.ShapeDtypeStruct((tokens, 2 * HEAD_DIM), F32)] * 2, [], [part], mib=32)
    return (d_hidden, d_route, d_queries, d_keys, d_values)


def solution(mesh):
    placed = (
        P("context", None),
        P("context", None),
        P(),
        P("context", None),
        P("context", None),
        P("context", None, "expert"),
        P("context", None, "expert"),
        P("context", "expert", None),
        P("expert", None),
        P("context", "expert"),
        P("context", None),
        P("context", None),
    )
    return jax.shard_map(
        body,
        mesh=mesh,
        in_specs=placed,
        out_specs=(
            P("context", None),
            P("context", None),
            P("context", "expert"),
            P("context", None),
            P("context", None),
        ),
        check_vma=False,
    )
```

```python
import math

import jax
import jax.numpy as jnp
from jax import lax
from jax.experimental import pallas as pl
from jax.experimental.pallas import tpu as pltpu
from jax.sharding import PartitionSpec as P

HEAD_DIM = 128
CAP = 12
BF = jnp.bfloat16
F32 = jnp.float32
PAIR = 2 * CAP
EPS = 1e-06
SCALE = 1.0 / math.sqrt(HEAD_DIM)
NT = (((1,), (1,)), ((), ()))
TN = (((0,), (0,)), ((), ()))
MB = 1 << 20
NEAR_MIB = 60
PACK_ROWS = 1024
PICK_COST = 30000000000
NEAR_TYPE = BF
NEAR_ROWS = 384
FAR_ROWS = 384
GRADS_MIB = 36
FINISH_MIB = 32
FAR_MIB = 60


def nt(a, b):
    return lax.dot_general(a, b, NT, preferred_element_type=F32)


def tn(a, b):
    return lax.dot_general(a, b, TN, preferred_element_type=F32)


def nn(a, b):
    return jnp.dot(a, b, preferred_element_type=F32)


def params(mib=60):
    return pltpu.CompilerParams(vmem_limit_bytes=mib * MB)


def whole(shape):
    return pl.BlockSpec(shape, lambda *_: (0,) * len(shape))


def row_expert(quarter, per, count, shape):
    row = lax.broadcasted_iota(jnp.int32, shape, 0)
    return jnp.where(row < count, row * per + quarter, -1)


def slot_split(shape, axis, first):
    slot = (lax.broadcasted_iota(jnp.int32, shape, axis) + first).astype(F32)
    lane = jnp.floor((slot + 0.5) * (1.0 / PAIR))
    rank = slot - PAIR * lane
    half = jnp.where(rank > CAP - 0.5, 1.0, 0.0)
    return lane, half, rank - CAP * half


def route_kernel(rows, per, count, q_ref, ids_ref, rw_ref, hid_ref, up_ref, gain_ref,
                 send_ref, picks_ref, m_ref, r_ref, w_ref, n_ref):
    step = pl.program_id(0)
    tokens = ids_ref.shape[1]

    @pl.when(step == 0)
    def _():
        ids = ids_ref[...]
        weights = rw_ref[...].astype(F32)
        named = row_expert(q_ref[0], per, count, (128, tokens))
        member = jnp.zeros((128, tokens), F32)
        weight = jnp.zeros((128, tokens), F32)
        for k in range(ids.shape[0]):
            hit = ids[k : k + 1] == named
            member = member + jnp.where(hit, 1.0, 0.0)
            weight = weight + jnp.where(hit, weights[k : k + 1], 0.0)
        m_ref[...] = member.astype(BF)
        w_ref[...] = weight.astype(BF)
        row = lax.broadcasted_iota(jnp.int32, (tokens, tokens), 0)
        col = lax.broadcasted_iota(jnp.int32, (tokens, tokens), 1)
        before = jnp.where(row < col, 1.0, 0.0).astype(BF)
        r_ref[...] = nn(member.astype(BF), before).astype(BF)
        wide = hid_ref[...].astype(F32)
        inv = lax.rsqrt(jnp.mean(wide * wide, axis=1, keepdims=True) + EPS)
        n_ref[:tokens] = (wide * inv * gain_ref[...]).astype(BF)
        n_ref[tokens:] = up_ref[...]

    lane_of, half_of, rank_of = slot_split((rows, 128), 0, step * rows)
    lane = lax.broadcasted_iota(jnp.int32, (rows, 128), 1).astype(F32)
    spread = jnp.where(lane == lane_of, 1.0, 0.0).astype(BF)
    chosen = (nn(spread, m_ref[...]) > 0.5) & (nn(spread, r_ref[...]) == rank_of)
    weight = nn(spread, w_ref[...])
    first, second = chosen & (half_of < 0.5), chosen & (half_of > 0.5)
    s0 = jnp.where(first, 1.0, 0.0).astype(BF)
    s1 = jnp.where(second, 1.0, 0.0).astype(BF)
    send_ref[...] = nn(jnp.concatenate([s0, s1], axis=1), n_ref[...]).astype(BF)
    picks_ref[:, :128] = jnp.where(first, weight, 0.0).astype(BF)
    picks_ref[:, 128:256] = jnp.where(second, weight, 0.0).astype(BF)
    picks_ref[:, 256:] = s0


def route(quarter, per, count, ids, weights, hidden, upstream, gain):
    tokens, width = hidden.shape
    rows = 256
    slots = count * PAIR
    return pl.pallas_call(
        lambda *refs: route_kernel(rows, per, count, *refs),
        grid_spec=pltpu.PrefetchScalarGridSpec(
            num_scalar_prefetch=1,
            grid=(slots // rows,),
            in_specs=[
                whole(ids.shape),
                whole(ids.shape),
                whole((tokens, width)),
                whole((tokens, width)),
                whole((1, width)),
            ],
            out_specs=[
                pl.BlockSpec((rows, width), lambda i, p: (i, 0)),
                pl.BlockSpec((rows, 3 * tokens), lambda i, p: (i, 0)),
            ],
            scratch_shapes=[
                pltpu.VMEM((128, tokens), BF),
                pltpu.VMEM((128, tokens), BF),
                pltpu.VMEM((128, tokens), BF),
                pltpu.VMEM((2 * tokens, width), BF),
            ],
        ),
        out_shape=[jax.ShapeDtypeStruct((slots, width), BF), jax.ShapeDtypeStruct((slots, 3 * tokens), BF)],
        compiler_params=params(),
        name="route",
    )(quarter, ids, weights, hidden, upstream, gain)


def pack_kernel(count, q_ref, g_ref, u_ref, d_ref, *refs):
    out_refs = refs[:count]
    tall_ref, down_ref, in_sems, out_sems = refs[count:]
    unit = g_ref.shape[2]
    blocks = d_ref.shape[2] // unit
    loads, stores = [], []
    for n, out in enumerate(out_refs):
        which = q_ref[n]
        pairs = [(g_ref.at[which], tall_ref.at[n, 0]), (u_ref.at[which], tall_ref.at[n, 1]), (d_ref.at[which], down_ref.at[n])]
        loads += [pltpu.make_async_copy(src, dst, in_sems.at[3 * n + k]) for k, (src, dst) in enumerate(pairs)]
        pairs = [[(tall_ref.at[n, k], out.at[k])] for k in range(2)]
        at = [pl.ds(k * unit, unit) for k in range(blocks)]
        pairs.append([(down_ref.at[n, :, span], out.at[2, span]) for span in at])
        for group in pairs:
            first = sum([len(g) for g in stores])
            stores.append([pltpu.make_async_copy(src, dst, out_sems.at[first + k]) for k, (src, dst) in enumerate(group)])
    for load in loads:
        load.start()
    for load, group in zip(loads, stores):
        load.wait()
        for store in group:
            store.start()
    for group in stores:
        for store in group:
            store.wait()


def pack(which, w_gate, w_up, w_down):
    width, unit = w_gate.shape[1:]
    count = which.shape[0]
    hbm = pl.BlockSpec(memory_space=pltpu.HBM)
    return pl.pallas_call(
        lambda *refs: pack_kernel(count, *refs),
        in_specs=[pl.BlockSpec(memory_space=pltpu.SMEM), hbm, hbm, hbm],
        out_specs=[hbm] * count,
        out_shape=[jax.ShapeDtypeStruct((3, width, unit), BF)] * count,
        scratch_shapes=[
            pltpu.VMEM((count, 2, width, unit), BF),
            pltpu.VMEM((count, unit, width), BF),
            pltpu.SemaphoreType.DMA((3 * count,)),
            pltpu.SemaphoreType.DMA((count * (2 + width // unit),)),
        ],
        compiler_params=params(),
        name="pack",
    )(which, w_gate, w_up, w_down)


def pick_kernel(q_ref, w_ref, out_ref):
    out_ref[...] = w_ref[...]


def pick(which, w):
    _, unit, width = w.shape
    return pl.pallas_call(
        pick_kernel,
        grid_spec=pltpu.PrefetchScalarGridSpec(
            num_scalar_prefetch=1,
            grid=(1,),
            in_specs=[pl.BlockSpec((1, unit, width), lambda i, q: (q[0], 0, 0))],
            out_specs=whole((1, unit, width)),
        ),
        out_shape=jax.ShapeDtypeStruct((1, unit, width), BF),
        cost_estimate=pl.CostEstimate(flops=PICK_COST, bytes_accessed=2 * unit * width * 2, transcendentals=0),
        compiler_params=params(),
        name="pick",
    )(which, w)


def unpack(ref):
    unit = ref.shape[2]
    down = [ref[2, n * unit : (n + 1) * unit] for n in range(ref.shape[1] // unit)]
    return ref[0], ref[1], jnp.concatenate(down, axis=1)


def expert_rows(xy, w_in, w_down):
    rows, width = xy.shape
    half_width = width // 2
    ahead = nn(xy, w_in)
    gate, up = ahead[:, : w_in.shape[1] // 2], ahead[:, w_in.shape[1] // 2 :]
    proj = pltpu.roll(nt(xy, w_down), rows - CAP, 0)
    sig = 1.0 / (1.0 + jnp.exp(-gate))
    silu = gate * sig
    act = (silu * up).astype(BF).astype(F32)
    d_gate = (proj * up * (sig * (1.0 + gate * (1.0 - sig)))).astype(BF)
    d_up = (proj * silu).astype(BF)
    d_route = jnp.sum(act * proj, axis=1, keepdims=True)
    d_rows = nt(jnp.concatenate([d_gate, d_up], axis=1), w_in)
    _, half, _ = slot_split((rows, 1), 0, 0)
    out = jnp.where(half > 0.5, pltpu.roll(d_rows[:, half_width:], CAP, 0), d_rows[:, :half_width])
    return out, jnp.broadcast_to(d_route, (rows, 128))


def near_kernel(rows, q_ref, xy_ref, go_ref, uo_ref, do_ref, a_ref, b_ref, out_ref):
    width = xy_ref.shape[1]
    one, two = unpack(a_ref), unpack(b_ref)
    w_in = jnp.concatenate([go_ref[0], one[0], two[0], uo_ref[0], one[1], two[1]], axis=1)
    w_down = jnp.concatenate([do_ref[0], one[2], two[2]], axis=0)
    out, d_route = expert_rows(xy_ref[...], w_in, w_down)
    out_ref[:, : width // 2] = out.astype(NEAR_TYPE)
    out_ref[:, width // 2 :] = d_route.astype(NEAR_TYPE)


def expert_near(quarter, xy, w_gate, w_up, own_down, got_a, got_b):
    slots, width = xy.shape
    unit = w_gate.shape[2]
    rows = NEAR_ROWS
    own = pl.BlockSpec((1, width, unit), lambda i, p: (p[0], 0, 0))
    narrow = width // 2 + 128
    return pl.pallas_call(
        lambda *refs: near_kernel(rows, *refs),
        grid_spec=pltpu.PrefetchScalarGridSpec(
            num_scalar_prefetch=1,
            grid=(slots // rows,),
            in_specs=[
                pl.BlockSpec((rows, width), lambda i, p: (i, 0)),
                own,
                own,
                whole((1, unit, width)),
                whole(got_a.shape),
                whole(got_b.shape),
            ],
            out_specs=pl.BlockSpec((rows, narrow), lambda i, p: (i, 0)),
        ),
        out_shape=jax.ShapeDtypeStruct((slots, narrow), NEAR_TYPE),
        compiler_params=params(NEAR_MIB),
        name="expert_near",
    )(quarter, xy, w_gate, w_up, own_down, got_a, got_b)


def far_kernel(xy_ref, in_ref, down_ref, near_ref, out_ref):
    width = xy_ref.shape[1]
    out, d_route = expert_rows(xy_ref[...], jnp.concatenate([in_ref[0], in_ref[1]], axis=1), down_ref[0])
    out_ref[:, : width // 2] = (near_ref[:, : width // 2] + out).astype(BF)
    out_ref[:, width // 2 :] = (near_ref[:, width // 2 :] + d_route).astype(BF)


def expert_far(xy, w_in, w_down, near):
    slots, width = xy.shape
    narrow = near.shape[1]
    rows = FAR_ROWS
    block = pl.BlockSpec((rows, narrow), lambda i: (i, 0))
    return pl.pallas_call(
        far_kernel,
        grid=(slots // rows,),
        in_specs=[pl.BlockSpec((rows, width), lambda i: (i, 0)), whole(w_in.shape), whole(w_down.shape), block],
        out_specs=block,
        out_shape=jax.ShapeDtypeStruct((slots, narrow), BF),
        compiler_params=params(FAR_MIB),
        name="expert_far",
    )(xy, w_in, w_down, near)


def gather_kernel(per, count, q_ref, back_ref, picks_ref, ids_ref, hid_ref, gain_ref, out_ref):
    tokens, width = hid_ref.shape
    half_width = width // 2
    wide = hid_ref[...].astype(F32)
    inv = lax.rsqrt(jnp.mean(wide * wide, axis=1, keepdims=True) + EPS)
    rows = back_ref[:, :half_width]
    halves = tn(picks_ref[:, : 2 * tokens], rows)
    d_normed = jnp.concatenate([halves[:tokens], halves[tokens:]], axis=1)
    g = d_normed * gain_ref[...]
    inner = jnp.mean(g * wide, axis=1, keepdims=True)
    out_ref[:, :width] = (inv * g - wide * (inv * inv * inv * inner)).astype(BF)
    slots = back_ref.shape[0]
    lane_of, _, _ = slot_split((slots, 128), 0, 0)
    lane = lax.broadcasted_iota(jnp.int32, (slots, 128), 1).astype(F32)
    placed = jnp.where(lane == lane_of, back_ref[:, half_width:].astype(F32), 0.0).astype(BF)
    route = tn(placed, picks_ref[:, 2 * tokens :])
    named = row_expert(q_ref[0], per, count, (128, tokens))
    ids = ids_ref[...]
    row = lax.broadcasted_iota(jnp.int32, (128, tokens), 0)
    out = jnp.zeros((128, tokens), F32)
    for k in range(ids.shape[0]):
        value = jnp.sum(jnp.where(ids[k : k + 1] == named, route, 0.0), axis=0, keepdims=True)
        out = jnp.where(row == k, value, out)
    out_ref[:, width:] = out.T.astype(BF)


def on_chip(kernel, name, out_shape, scalars, arrays, scratch=(), mib=60):
    vmem = pl.BlockSpec(memory_space=pltpu.VMEM)
    many = isinstance(out_shape, list)
    return pl.pallas_call(
        kernel,
        in_specs=[pl.BlockSpec(memory_space=pltpu.SMEM)] * len(scalars) + [vmem] * len(arrays),
        out_specs=[vmem] * len(out_shape) if many else vmem,
        out_shape=out_shape,
        scratch_shapes=list(scratch),
        compiler_params=params(mib),
        name=name,
    )(*scalars, *arrays)


def sum_first(ref):
    total = ref[0].astype(F32)
    for n in range(1, ref.shape[0]):
        total = total + ref[n].astype(F32)
    return total


def finish_kernel(z_ref, in_ref, up_ref, out_ref):
    width = up_ref.shape[1]
    total = sum_first(in_ref)
    mine = up_ref[...].astype(F32)
    done = jnp.concatenate([total[:, :width] + mine, total[:, width:]], axis=1).astype(BF)
    for n in range(in_ref.shape[0]):
        out_ref[n] = done


def finish(z, arrived, upstream):
    parts, share, wide = arrived.shape
    return pl.pallas_call(
        finish_kernel,
        grid_spec=pltpu.PrefetchScalarGridSpec(
            num_scalar_prefetch=1,
            grid=(1,),
            in_specs=[
                whole((parts, share, wide)),
                pl.BlockSpec((share, upstream.shape[1]), lambda i, z: (z[0], 0)),
            ],
            out_specs=whole((parts, share, wide)),
        ),
        out_shape=jax.ShapeDtypeStruct((parts, share, wide), BF),
        compiler_params=params(FINISH_MIB),
        name="finish_hidden",
    )(z, arrived, upstream)


def spread_kernel(in_ref, out_ref):
    total = sum_first(in_ref).astype(BF)
    for n in range(out_ref.shape[0]):
        out_ref[n] = total


def last_kernel(in_ref, dk_ref, dv_ref):
    half = in_ref.shape[0] // 2
    for head in range(2):
        total = in_ref[head * half].astype(F32)
        for n in range(1, half):
            total = total + in_ref[head * half + n].astype(F32)
        at = slice(head * HEAD_DIM, (head + 1) * HEAD_DIM)
        dk_ref[:, at] = total[:, :HEAD_DIM]
        dv_ref[:, at] = total[:, HEAD_DIM:]


def heads_to_rows(x):
    return jnp.concatenate([x[:, :HEAD_DIM], x[:, HEAD_DIM:]], axis=0)


def probs_kernel(chunk, q_ref, o_ref, kv_ref, p_ref, stat_ref, s_ref):
    query = jnp.concatenate([heads_to_rows(q_ref[...]), heads_to_rows(o_ref[...])], axis=0)
    count = query.shape[0]
    steps = [slice(n, n + chunk) for n in range(0, kv_ref.shape[0], chunk)]
    top = None
    for span in steps:
        s = nt(kv_ref[span, :HEAD_DIM], query) * SCALE
        s_ref[span] = s
        most = jnp.max(s, axis=0, keepdims=True)
        top = most if top is None else jnp.maximum(top, most)
    total = jnp.zeros_like(top)
    out = jnp.zeros((HEAD_DIM, count), F32)
    for span in steps:
        e = jnp.exp(s_ref[span] - top)
        total = total + jnp.sum(e, axis=0, keepdims=True)
        p = e.astype(BF)
        p_ref[span] = p
        out = out + tn(kv_ref[span, HEAD_DIM:], p)
    stat_ref[:HEAD_DIM] = out
    row = lax.broadcasted_iota(jnp.int32, (8, count), 0)
    stat_ref[HEAD_DIM:] = jnp.where(row == 0, top, total)


def probs(queries, other, kv):
    count = kv.shape[0]
    rows = queries.shape[0] * 4
    return on_chip(
        lambda *refs: probs_kernel(512, *refs), "attention_probs",
        [jax.ShapeDtypeStruct((count, rows), BF), jax.ShapeDtypeStruct((HEAD_DIM + 8, rows), F32)],
        [], [queries, other, kv], [pltpu.VMEM((count, rows), F32)], mib=60)


def grads_kernel(chunk, dh_ref, do_ref, w_ref, q_ref, o_ref, p_ref, stat_ref, far_ref, kv_ref, dq_ref, dqo_ref, dkv_ref):
    width = w_ref.shape[1]
    tokens = dh_ref.shape[0]
    d_hidden = jnp.concatenate([dh_ref[:, :width], do_ref[:, :width]], axis=0)
    d_out_w = nt(w_ref[...], d_hidden).astype(BF)
    parts = [d_out_w[h * HEAD_DIM : (h + 1) * HEAD_DIM, c * tokens : (c + 1) * tokens] for c in range(2) for h in range(2)]
    d_out_t = jnp.concatenate(parts, axis=1)
    d_out = jnp.concatenate([p.T for p in parts], axis=0)
    query = jnp.concatenate([heads_to_rows(q_ref[...]), heads_to_rows(o_ref[...])], axis=0)
    half = query.shape[0] // 2
    here = stat_ref[...]
    there = jnp.concatenate([far_ref[:, half:], far_ref[:, :half]], axis=1)
    top_here, top_there = here[HEAD_DIM : HEAD_DIM + 1], there[HEAD_DIM : HEAD_DIM + 1]
    top = jnp.maximum(top_here, top_there)
    in_here, in_there = jnp.exp(top_here - top), jnp.exp(top_there - top)
    total = here[HEAD_DIM + 1 : HEAD_DIM + 2] * in_here + there[HEAD_DIM + 1 : HEAD_DIM + 2] * in_there
    in_here, in_there = in_here / total, in_there / total
    out = here[:HEAD_DIM] * in_here + there[:HEAD_DIM] * in_there
    delta = jnp.sum(d_out_t.astype(F32) * out, axis=0, keepdims=True)
    d_query = jnp.zeros((HEAD_DIM, 2 * half), F32)
    for n in range(0, kv_ref.shape[0], chunk):
        span = slice(n, n + chunk)
        p = p_ref[span].astype(F32) * in_here
        d_probs = nn(kv_ref[span, HEAD_DIM:], d_out_t)
        ds = (p * (d_probs - delta)).astype(BF)
        dkv_ref[span, :HEAD_DIM] = (nn(ds, query) * SCALE).astype(BF)
        dkv_ref[span, HEAD_DIM:] = nn(p.astype(BF), d_out).astype(BF)
        d_query = d_query + tn(kv_ref[span, :HEAD_DIM], ds)
    d_query = (d_query * SCALE).T
    for ref, at in ((dq_ref, 0), (dqo_ref, half)):
        ref[:, :HEAD_DIM] = d_query[at : at + tokens]
        ref[:, HEAD_DIM:] = d_query[at + tokens : at + 2 * tokens]


def body(hidden, upstream, norm_gain, route_ids, route_weights, w_gate, w_up, w_down, w_out, queries, keys, values):
    ctx_count = lax.axis_size("context")
    exp_count = lax.axis_size("expert")
    tokens, width = hidden.shape
    chips = ctx_count // 2
    per = w_gate.shape[0]
    slots = ctx_count * PAIR
    z = lax.axis_index("expert")
    quarter = z % per
    q_arr = quarter.astype(jnp.int32).reshape(1)
    z_arr = z.astype(jnp.int32).reshape(1)
    gain = norm_gain.reshape(1, width)
    swap_core = [(i, i ^ 1) for i in range(ctx_count)]
    same_core = [[2 * i + k for i in range(chips)] for k in range(2)]

    def far(core):
        return -2 if core == 0 else 2

    def moves(step):
        return [
            (i * ctx_count + c, (i + step(c % 2)) % exp_count * ctx_count + c)
            for c in range(ctx_count)
            for i in range(exp_count)
        ]

    def trade(w, step):
        return lax.ppermute(w, ("expert", "context"), moves(step))

    leave = jnp.stack([((z + n) % per).astype(jnp.int32) for n in (1, per - 1)])
    near_a, near_b = pack(leave, w_gate, w_up, w_down)
    near_a, near_b = trade(near_a, lambda core: 1), trade(near_b, lambda core: -1)
    far_gate, far_up, far_down = [lax.dynamic_slice_in_dim(w, (z + 2) % per, 1, 0) for w in (w_gate, w_up, w_down)]
    far_in = trade(jnp.concatenate([far_gate, far_up], axis=0), far)
    far_down = trade(far_down, far)
    mine, near_a, near_b = lax.optimization_barrier((q_arr, near_a, near_b))
    own_down = pick(mine, w_down)

    ids = route_ids.T
    kv_head = z // (exp_count // 2)
    own_kv = jnp.concatenate(
        [lax.dynamic_slice_in_dim(a, kv_head * HEAD_DIM, HEAD_DIM, 1) for a in (keys, values)], axis=1)
    kv = lax.all_gather(own_kv, "context", axis=0, tiled=True, axis_index_groups=same_core)

    send, picks = route(q_arr, per, ctx_count, ids, route_weights.T, hidden, upstream, gain)
    xy = lax.all_to_all(send.reshape(ctx_count, PAIR, width), "context", 0, 0, tiled=True)
    xy = xy.reshape(slots, width)
    narrow = width // 2 + 128
    near = expert_near(q_arr, xy, w_gate, w_up, own_down, near_a, near_b)
    rows = expert_far(xy, far_in, far_down, near)
    rows, kv = lax.optimization_barrier((rows, kv))
    rows = lax.all_to_all(rows.reshape(ctx_count, PAIR, narrow), "context", 0, 0, tiled=True)
    wide = width + 128
    q = on_chip(
        lambda *refs: gather_kernel(per, ctx_count, *refs), "gather_rows",
        jax.ShapeDtypeStruct((tokens, wide), BF),
        [q_arr], [rows.reshape(slots, narrow), picks, ids, hidden, gain], mib=36)

    share = tokens // exp_count
    parts = (exp_count, share, wide)
    arrived = lax.all_to_all(q.reshape(parts), "expert", 0, 0, tiled=True)
    queries, q = lax.optimization_barrier((queries, q))
    other = lax.ppermute(queries, "context", swap_core)
    soft, stats = probs(queries, other, kv)
    far_stats = lax.ppermute(stats, "context", swap_core)
    arrived, far_stats = lax.optimization_barrier((arrived, far_stats))
    done = finish(z_arr, arrived, upstream)
    done = lax.all_to_all(done, "expert", 0, 0, tiled=True).reshape(tokens, wide)
    d_hidden = done[:, :width]
    d_route = done[:, width : width + route_ids.shape[1]].astype(F32)

    done_other = lax.ppermute(done, "context", swap_core)
    d_queries, d_other, part = on_chip(
        lambda *refs: grads_kernel(512, *refs), "attention_grads",
        [
            jax.ShapeDtypeStruct(queries.shape, F32),
            jax.ShapeDtypeStruct(queries.shape, F32),
            jax.ShapeDtypeStruct(kv.shape, BF),
        ],
        [], [done, done_other, w_out, queries, other, soft, stats, far_stats, kv], mib=GRADS_MIB)
    d_queries = d_queries + lax.ppermute(d_other, "context", swap_core)
    part = lax.all_to_all(
        part.reshape(chips, tokens, 2 * HEAD_DIM), "context", 0, 0, tiled=True, axis_index_groups=same_core)
    block = (exp_count, tokens, 2 * HEAD_DIM)
    part = on_chip(spread_kernel, "sum_chips", jax.ShapeDtypeStruct(block, BF), [], [part], mib=32)
    part = lax.all_to_all(part, "expert", 0, 0, tiled=True)
    d_keys, d_values = on_chip(
        last_kernel, "sum_heads", [jax.ShapeDtypeStruct((tokens, 2 * HEAD_DIM), F32)] * 2, [], [part], mib=32)
    return (d_hidden, d_route, d_queries, d_keys, d_values)


def solution(mesh):
    placed = (
        P("context", None),
        P("context", None),
        P(),
        P("context", None),
        P("context", None),
        P("context", None, "expert"),
        P("context", None, "expert"),
        P("context", "expert", None),
        P("expert", None),
        P("context", "expert"),
        P("context", None),
        P("context", None),
    )
    return jax.shard_map(
        body,
        mesh=mesh,
        in_specs=placed,
        out_specs=(
            P("context", None),
            P("context", None),
            P("context", "expert"),
            P("context", None),
            P("context", None),
        ),
        check_vma=False,
    )
```
